512 devices in a mesh: lat: 16 (over x_lo, z), lon: 32 (over x_hi, y, core).
Axes of the slice: x: 4 (x_hi: 2, x_lo: 2; x = x_hi * 2 + x_lo), y: 8, z: 8, core: 2. Of those that a mesh axis runs over, the one named last changes fastest.
Arguments:
- query_field: bfloat16 [1, 256, 512, 512], P(None, 'lat', 'lon'), may hold values from -6 to 6
- key_field: bfloat16 [1, 256, 512, 512], P(None, 'lat', 'lon'), may hold values from -6 to 6
- value_field: bfloat16 [1, 256, 512, 512], P(None, 'lat', 'lon'), may hold values from -6 to 6
- out_grad: bfloat16 [1, 256, 512, 1024], P(None, 'lat', 'lon'), may hold values from -6 to 6
- out_weight: bfloat16 [512, 1024], P('lat', 'lon'), may hold values from -0.25 to 0.25
- time_weight: bfloat16 [256, 1024], replicated, may hold values from -0.375 to 0.375
- rel_bias: float32 [8, 49], replicated, may hold values from -4 to 4
- timesteps: int32 [1], replicated, may hold values from 0 to 999
Outputs:
- query_grad: bfloat16 [1, 256, 512, 512], P(None, 'lat', 'lon')
- key_grad: bfloat16 [1, 256, 512, 512], P(None, 'lat', 'lon')
- value_grad: bfloat16 [1, 256, 512, 512], P(None, 'lat', 'lon')
- out_weight_grad: float32 [512, 1024], P('lat', 'lon')
- time_weight_grad: float32 [256, 1024], P('lat', 'lon')
- bias_grad: float32 [8, 49], replicated
The draws below stay inside these ranges and needn't reach their ends.
All inputs are finite; a program needn't handle non-finite values.
Results may differ from the reference program's by a relative error of at most 0.022.
Values may be sent and summed in bfloat16 or wider, within the bound.
A program may use at most 128 MiB of HBM per device.

```python
import math
import jax
import jax.numpy as jnp
from jax import lax

C = 1024
HEADS = 8
HEAD_DIM = 64
EMB = 256
STEPS = 1000
SHIFT = 2
FRAMES = 1
HD = 512
LAT = 256
LON = 512


def draw_query_field(key, part):
    key = jax.random.fold_in(key, 11)
    drawn = jnp.clip(jax.random.normal(key, (FRAMES, LAT, LON, HEADS * HEAD_DIM), jnp.float32), -6.0, 6.0)
    return drawn.astype(jnp.bfloat16)


def draw_key_field(key, part):
    key = jax.random.fold_in(key, 12)
    drawn = jnp.clip(jax.random.normal(key, (FRAMES, LAT, LON, HEADS * HEAD_DIM), jnp.float32), -6.0, 6.0)
    return drawn.astype(jnp.bfloat16)


def block_scale(stream_key, extent, cuts, smallest, high):
    factor_of, own = 1.0, jax.random.fold_in(stream_key, 6)
    for axis_at, blocks in cuts:
        draws = jnp.exp(jax.random.uniform(jax.random.fold_in(own, axis_at), (blocks,), jnp.float32, smallest / len(cuts), high / len(cuts)))
        factor_of = factor_of * jnp.repeat(draws, extent[axis_at] // blocks).reshape([-1 if axis == axis_at else 1 for axis in range(len(extent))])
    return factor_of


def normal_values(key, dims, scale, most, cuts=(), kind=jnp.bfloat16):
    factor_of = block_scale(key, dims, cuts, -0.22, 0.18) if cuts else 1.0
    values = jax.random.normal(key, dims, jnp.float32) * scale * factor_of
    return jnp.minimum(jnp.maximum(values, -most), most).astype(kind)


def setup_inputs(seed: int = 0) -> dict:
    streams_of = jax.random.split(jax.random.key(seed), 9)
    return {
        "query_field": draw_query_field(jax.random.fold_in(streams_of[8], 71), 0),
        "key_field": draw_key_field(jax.random.fold_in(streams_of[8], 71), 0),
        "value_field": normal_values(streams_of[2], (FRAMES, LAT, LON, HD), 1.0, 6.0, ((1, 16), (2, 32))),
        "out_grad": normal_values(streams_of[3], (FRAMES, LAT, LON, C), 1.0, 6.0, ((1, 16), (2, 32))),
        "out_weight": normal_values(streams_of[4], (HD, C), HD ** -0.5, 0.25, ((0, 16), (1, 32))),
        "time_weight": normal_values(streams_of[5], (EMB, C), EMB ** -0.5, 0.375),
        "rel_bias": normal_values(streams_of[6], (HEADS, 49), 1.0, 4.0, (), jnp.float32),
        "timesteps": jax.random.randint(streams_of[7], (FRAMES,), 0, STEPS).astype(jnp.int32),
    }


def bucket_table():
    slots = jnp.arange(16, dtype=jnp.int32)
    row_gap = slots[:, None] // 4 - slots[None, :] // 4 + 3
    col_gap = slots[:, None] % 4 - slots[None, :] % 4 + 3
    index = (row_gap * 7 + col_gap).reshape(256)
    return (index[:, None] == jnp.arange(49, dtype=jnp.int32)[None, :]).astype(jnp.float32)

def time_embed(timesteps, width):
    half = width // 2
    freqs = jnp.exp(-math.log(10000.0) * jnp.arange(half, dtype=jnp.float32) / half)
    angles = timesteps.astype(jnp.float32)[:, None] * freqs[None, :]
    return jnp.concatenate([jnp.cos(angles), jnp.sin(angles)], axis=1)

def to_windows(field, heads):
    rows, cols, width = field.shape
    shaped = field.reshape(rows // 4, 4, cols // 4, 4, heads, width // heads)
    return shaped.transpose(0, 2, 1, 3, 4, 5).reshape(-1, 16, heads, width // heads)

def mask_windows(flags):
    rows, cols = flags.shape
    return flags.reshape(rows // 4, 4, cols // 4, 4).transpose(0, 2, 1, 3).reshape(-1, 16)

def from_windows(windows, rows, cols):
    heads, depth = (windows.shape[2], windows.shape[3])
    shaped = windows.reshape(rows // 4, cols // 4, 4, 4, heads, depth)
    return shaped.transpose(0, 2, 1, 3, 4, 5).reshape(rows, cols, heads * depth)

def window_pass(query_win, key_win, value_win, cot_win, key_ok, bias_full, scale):
    f32 = jnp.float32
    scores = jnp.einsum('wqhd,wkhd->whqk', query_win.astype(f32), key_win.astype(f32)) * scale + bias_full[None]
    scores = jnp.where(key_ok[:, None, None, :], scores, -1000000000.0)
    top = lax.optimization_barrier(jnp.max(scores, axis=-1, keepdims=True))
    expo = jnp.exp(scores - top)
    probs = expo / lax.optimization_barrier(jnp.sum(expo, axis=-1, keepdims=True))
    probs_b = probs.astype(jnp.bfloat16)
    attn = jnp.einsum('whqk,wkhd->wqhd', probs_b.astype(f32), value_win.astype(f32)).astype(jnp.bfloat16)
    dvalue = jnp.einsum('whqk,wqhd->wkhd', probs_b.astype(f32), cot_win.astype(f32)).astype(jnp.bfloat16)
    dprob = jnp.einsum('wqhd,wkhd->whqk', cot_win.astype(f32), value_win.astype(f32))
    dscore = probs * (dprob - lax.optimization_barrier(jnp.sum(probs * dprob, axis=-1, keepdims=True)))
    dscore_b = dscore.astype(jnp.bfloat16).astype(f32)
    dquery = (jnp.einsum('whqk,wkhd->wqhd', dscore_b, key_win.astype(f32)) * scale).astype(jnp.bfloat16)
    dkey = (jnp.einsum('whqk,wqhd->wkhd', dscore_b, query_win.astype(f32)) * scale).astype(jnp.bfloat16)
    return (attn, dquery, dkey, dvalue, dscore)

def reference(query_field, key_field, value_field, out_grad, out_weight, time_weight, rel_bias, timesteps):
    f32 = jnp.float32
    high = lax.Precision.HIGHEST
    emb = time_embed(timesteps, EMB)
    gate = jnp.dot(emb, time_weight.astype(f32), precision=high)
    table = bucket_table()
    bias_full = jnp.dot(rel_bias, table.T, precision=high).reshape(HEADS, 16, 16)
    scale = HEAD_DIM ** (-0.5)
    rows_region = LAT + 4

    def region(field):
        field = jnp.roll(field, -SHIFT, axis=1)
        return jnp.pad(field, ((SHIFT, 4 - SHIFT), (0, 0), (0, 0)))

    def back(windows):
        field = from_windows(windows, rows_region, LON)
        return jnp.roll(field[SHIFT:SHIFT + LAT], SHIFT, axis=1)
    rows = jnp.arange(rows_region, dtype=jnp.int32) - SHIFT
    valid = (rows >= 0) & (rows < LAT)
    valid_grid = jnp.broadcast_to(valid[:, None], (rows_region, LON))

    def one_frame(items):
        query, key, value, grad, gate_row = items
        g = (grad.astype(f32) * gate_row).astype(jnp.bfloat16)
        dattn = jnp.dot(g.reshape(-1, C), out_weight.T, preferred_element_type=f32).astype(jnp.bfloat16).reshape(LAT, LON, HD)
        cot = jnp.where(valid[:, None, None], region(dattn), jnp.zeros((), jnp.bfloat16))
        attn_w, dq_w, dk_w, dv_w, dscore = window_pass(to_windows(region(query), HEADS), to_windows(region(key), HEADS), to_windows(region(value), HEADS), to_windows(cot, HEADS), mask_windows(valid_grid), bias_full, scale)
        dbias = jnp.dot(lax.optimization_barrier(jnp.sum(dscore, axis=0)).reshape(HEADS, 256), table, precision=high)
        attn = back(attn_w).reshape(-1, HD)
        proj = jnp.dot(attn, out_weight, preferred_element_type=f32)
        dgate = lax.optimization_barrier(jnp.sum(grad.astype(f32).reshape(-1, C) * proj, axis=0))
        dweight = jnp.dot(attn.T, g.reshape(-1, C), preferred_element_type=f32)
        return (back(dq_w), back(dk_w), back(dv_w), dweight, dgate, dbias)
    outs = lax.map(one_frame, (query_field, key_field, value_field, out_grad, gate))
    factor = 1.0 / math.sqrt(FRAMES * LAT * LON)
    weight_grad = lax.optimization_barrier(jnp.sum(outs[3], axis=0)) * factor
    gate_grad = outs[4] * factor
    time_grad = jnp.dot(emb.T, gate_grad, precision=high)
    bias_grad = lax.optimization_barrier(jnp.sum(outs[5], axis=0)) * factor
    return (outs[0], outs[1], outs[2], weight_grad, time_grad, bias_grad)
```

```python
import functools
import math

import jax
import jax.numpy as jnp
import numpy as np
from jax import lax
from jax.experimental import pallas as pl
from jax.experimental.pallas import tpu as pltpu
from jax.sharding import PartitionSpec as P

SHIFT = 2
XL = 2
XH = 2
NEG = -1e9
MESH = pl.DeviceIdType.MESH
BF = jnp.bfloat16
F32 = jnp.float32


def strip_tables():
    first = np.zeros((2, 7, 16, 256), np.float32)
    second = np.zeros((2, 7, 16, 256), np.float32)
    for way, col0 in ((0, 14), (1, 0)):
        for block in range(7):
            for r in range(4):
                if block < 5:
                    row = 4 * block + r - SHIFT
                elif block == 5:
                    row = 14 + r if r < 2 else -1
                else:
                    row = r - 2 if r >= 2 else -1
                if not 0 <= row < 16:
                    continue
                for c in range(2):
                    token = row * 16 + col0 + c
                    low = r * 2 + c
                    first[way, block, low if way == 0 else low + 8, token] = 1.0
                    second[way, block, low + 8 if way == 0 else low, token] = 1.0
    return first.reshape(224, 256), second.reshape(224, 256)


def slot_places(swap):
    places = [(i // 16, i % 16 + SHIFT) for i in range(64)]
    left = [(r, c) for r in range(4) for c in range(2)]
    right = [(r, 18 + c) for r in range(4) for c in range(2)]
    return places + (right + left if swap else left + right)


def place_tables():
    queries, keys = slot_places(False), slot_places(True)
    offsets = np.full((80, 80), 49, np.int32)
    for k, (kr, kc) in enumerate(keys):
        for q, (qr, qc) in enumerate(queries):
            if kc // 4 == qc // 4:
                offsets[k, q] = 7 * (qr - kr + 3) + (qc % 4 - kc % 4 + 3)
    fold_keys = np.zeros((32, 160), np.float32)
    for head in range(2):
        for k, (kr, kc) in enumerate(keys):
            fold_keys[head * 16 + kr * 4 + kc % 4, head * 80 + k] = 1.0
    fold_queries = np.zeros((80, 16), np.float32)
    for q, (qr, qc) in enumerate(queries):
        fold_queries[q, qr * 4 + qc % 4] = 1.0
    return offsets, fold_keys, fold_queries


def dot(a, b, ca, cb, precision=None):
    return lax.dot_general(
        a, b, (((ca,), (cb,)), ((), ())), precision=precision, preferred_element_type=F32
    )


def kernel(
    nz,
    ny,
    hd,
    model,
    factor,
    q_in,
    k_in,
    v_in,
    og_in,
    w_in,
    tw_in,
    rel_in,
    t_in,
    selq,
    selk,
    offs,
    foldk,
    foldq,
    dq_out,
    dk_out,
    dv_out,
    wg_out,
    tg_out,
    bg_out,
    xe,
    lrx,
    snd,
    rcv,
    slab,
    yb,
    wz,
    wf,
    ge,
    gate_ref,
    bias_ref,
    prob_ref,
    mb,
    rc,
    mc,
    rx,
    mz,
    rz,
    ry,
    rsum,
    dqs,
    dks,
    dvs,
    bterm,
    ay,
    az,
    ax,
    load_sem,
    out_sem,
    halo_s,
    halo_r,
    agy_s,
    agy_r,
    agz_s,
    agz_r,
    agx_s,
    agx_r,
    agc_s,
    agc_r,
    rsc_s,
    rsc_r,
    rsx_s,
    rsx_r,
    rsz_s,
    rsz_r,
    rsy_s,
    rsy_r,
    ary_s,
    ary_r,
    arz_s,
    arz_r,
    arx_s,
    arx_r,
):
    lat = lax.axis_index("lat")
    lon = lax.axis_index("lon")
    nlat, nlon = XL * nz, XH * ny * 2
    xl, z = lat // nz, lat % nz
    xh, y, core = lon // (2 * ny), (lon // 2) % ny, lon % 2
    half = model // XH
    slabs = hd // 128
    heads = hd // 64
    width = 3 * hd + model
    og0 = 3 * hd
    groups = ny // 2

    def at(xl_, z_, xh_, y_, core_):
        return (xl_ * nz + z_, xh_ * 2 * ny + y_ * 2 + core_)

    zs = [(d, lax.rem(z + d, nz), lax.rem(z - d + nz, nz)) for d in range(1, nz)]
    xs = [(a, b) for a in range(XL) for b in range(XH) if a + b]
    ys = [
        (dy, dc, lax.rem(y + dy, ny), lax.rem(y - dy + ny, ny), core ^ dc)
        for dy in range(ny)
        for dc in range(2)
        if dy + dc
    ]
    up, down = lax.rem(lat + nlat - 1, nlat), lax.rem(lat + 1, nlat)
    left, right = lax.rem(lon + nlon - 1, nlon), lax.rem(lon + 1, nlon)

    def remote(src, dst, send, recv, device):
        return pltpu.make_async_remote_copy(
            src_ref=src,
            dst_ref=dst,
            send_sem=send,
            recv_sem=recv,
            device_id=device,
            device_id_type=MESH,
        )

    loads = [
        pltpu.make_async_copy(q_in.at[0], xe.at[2:18, :, 0:hd], load_sem.at[0]),
        pltpu.make_async_copy(k_in.at[0], xe.at[2:18, :, hd : 2 * hd], load_sem.at[1]),
        pltpu.make_async_copy(v_in.at[0], xe.at[2:18, :, 2 * hd : og0], load_sem.at[2]),
        pltpu.make_async_copy(og_in.at[0], xe.at[2:18, :, og0:width], load_sem.at[3]),
    ]
    for load in loads:
        load.start()

    barrier = pltpu.get_barrier_semaphore()
    peers = [at(xl, z_, xh, y, core) for _, z_, _ in zs]
    peers += [at(xl ^ a, z, xh ^ b, y, core) for a, b in xs]
    peers += [at(xl, z, xh, y_, core_) for _, _, y_, _, core_ in ys]
    peers += [(up, lon), (down, lon)]
    peers += [(i, j) for j in (left, right) for i in (lat, up, down)]
    for peer in peers:
        pl.semaphore_signal(barrier, inc=1, device_id=peer, device_id_type=MESH)

    lane = lax.broadcasted_iota(jnp.int32, (32, 128), 1)
    row = lax.broadcasted_iota(jnp.int32, (32, 128), 0)
    lane0 = lax.rem(lon, 4) * 32
    spread = (lane == row + lane0).astype(F32).astype(BF)
    slab[...] = dot(w_in[...], spread, 1, 0).astype(BF).reshape(2, 16, 128)
    yb[y, core] = slab[core]

    for load in loads:
        load.wait()

    fields = [
        xe[2:18, :, 0:hd].reshape(256, hd),
        xe[2:18, :, hd : 2 * hd].reshape(256, hd),
        xe[2:18, :, og0 : og0 + half].reshape(256, hd),
        xe[2:18, :, 2 * hd : og0].reshape(256, hd),
        xe[2:18, :, og0 + half : width].reshape(256, hd),
    ]
    sq, sk = selq[...], selk[...]
    snd[:, :, 0] = (
        (dot(sq, fields[0], 1, 0) + dot(sk, fields[1], 1, 0)).astype(BF).reshape(2, 7, 16, hd)
    )
    snd[:, :, 1] = (
        (dot(sq, fields[2], 1, 0) + dot(sk, fields[3], 1, 0)).astype(BF).reshape(2, 7, 16, hd)
    )
    snd[:, :, 2] = dot(sq, fields[4], 1, 0).astype(BF).reshape(2, 7, 16, hd)

    pl.semaphore_wait(barrier, len(peers))

    def agy(dy, dc, y_, core_, yslot, cslot):
        return remote(
            slab.at[core_],
            yb.at[yslot, cslot],
            agy_s.at[dy, dc],
            agy_r.at[dy, dc],
            at(xl, z, xh, y_, core_),
        )

    agy_sent = [agy(dy, dc, y_, core_, y, core) for dy, dc, y_, _, core_ in ys]
    for copy in agy_sent:
        copy.start()

    halos = [
        remote(xe.at[16:18], xe.at[0:2], halo_s.at[0], halo_r.at[0], (down, lon)),
        remote(xe.at[2:4], xe.at[18:20], halo_s.at[1], halo_r.at[1], (up, lon)),
        remote(snd.at[0, 0:5], rcv.at[0, 0:5], halo_s.at[2], halo_r.at[2], (lat, right)),
        remote(snd.at[1, 0:5], rcv.at[1, 0:5], halo_s.at[3], halo_r.at[3], (lat, left)),
        remote(snd.at[0, 5], rcv.at[0, 5], halo_s.at[4], halo_r.at[4], (down, right)),
        remote(snd.at[0, 6], rcv.at[0, 6], halo_s.at[5], halo_r.at[5], (up, right)),
        remote(snd.at[1, 5], rcv.at[1, 5], halo_s.at[6], halo_r.at[6], (down, left)),
        remote(snd.at[1, 6], rcv.at[1, 6], halo_s.at[7], halo_r.at[7], (up, left)),
    ]
    for copy in halos:
        copy.start()

    tval = t_in[0].astype(F32)
    half_emb = tw_in.shape[0] // 2
    decay = -math.log(10000.0)
    freq = lax.broadcasted_iota(jnp.int32, (16, half_emb), 1).astype(F32)
    angle = tval * jnp.exp(decay * freq / half_emb)
    emb = jnp.concatenate([jnp.cos(angle), jnp.sin(angle)], axis=1)
    emb_hi = emb.astype(BF).astype(F32)
    emb_mid = (emb - emb_hi).astype(BF).astype(F32)
    emb_lo = emb - emb_hi - emb_mid
    emb_row = lax.broadcasted_iota(jnp.int32, (16, 2 * half_emb), 0)
    parts = jnp.where(
        emb_row == 0,
        emb_hi,
        jnp.where(emb_row == 1, emb_mid, jnp.where(emb_row == 2, emb_lo, 0.0)),
    ).astype(BF)
    gate = jnp.sum(dot(parts, tw_in[...], 1, 0), axis=0, keepdims=True)
    gate_ref[...] = jnp.broadcast_to(gate, (8, model))

    def bias_rows(i, carry):
        rows = pl.ds(pl.multiple_of(i * 16, 16), 16)
        code = offs[rows, :]
        acc = [jnp.full((16, 80), NEG, F32) for _ in range(heads)]
        for o in range(49):
            hit = code == o
            acc = [jnp.where(hit, rel_in[h, o], acc[h]) for h in range(heads)]
        for h in range(heads):
            bias_ref[h, rows, :] = acc[h]
        return carry

    lax.fori_loop(0, 5, bias_rows, 0)

    for dy, dc, _, ysrc, csrc in ys:
        agy(dy, dc, ysrc, csrc, ysrc, csrc).wait_recv()
    for g in range(groups):
        pair = yb[2 * g, 0] + yb[2 * g, 1] + (yb[2 * g + 1, 0] + yb[2 * g + 1, 1])
        wz[z, :, g * 128 : (g + 1) * 128] = pair

    def agz(d, z_, zslot):
        return remote(
            wz.at[zslot], wz.at[zslot], agz_s.at[d], agz_r.at[d], at(xl, z_, xh, y, core)
        )

    agz_sent = [agz(d, z_, z) for d, z_, _ in zs]
    for copy in agz_sent:
        copy.start()

    for copy in halos:
        copy.wait_recv()
    top = (lax.broadcasted_iota(jnp.int32, (16, hd), 0) < 8).astype(F32).astype(BF)
    bot = (lax.broadcasted_iota(jnp.int32, (16, hd), 0) >= 8).astype(F32).astype(BF)
    for wi in range(5):
        got = []
        for m in range(3):
            pair = [rcv[0, wi, m], rcv[1, wi, m]]
            if wi == 0:
                pair = [pair[0] + rcv[0, 5, m], pair[1] + rcv[1, 5, m]]
            if wi == 4:
                pair = [pair[0] + rcv[0, 6, m], pair[1] + rcv[1, 6, m]]
            got.append(pair)
        lrx[wi, :, 0:hd] = got[0][0] * top + got[0][1] * bot
        lrx[wi, :, hd : 2 * hd] = got[0][1] * top + got[0][0] * bot
        lrx[wi, :, 2 * hd : og0] = got[1][1] * top + got[1][0] * bot
        lrx[wi, :, og0 : og0 + half] = got[1][0] * top + got[1][1] * bot
        lrx[wi, :, og0 + half : width] = got[2][0] * top + got[2][1] * bot

    lanes = lax.broadcasted_iota(jnp.int32, (80, 128), 1)
    mask0 = (lanes < 64).astype(F32).astype(BF)
    mask1 = (lanes >= 64).astype(F32).astype(BF)
    low_lanes = lax.broadcasted_iota(jnp.int32, (64, 128), 1) < 64

    def slot_row(shape, dim):
        i = lax.broadcasted_iota(jnp.int32, shape, dim)
        return jnp.where(i < 64, i // 16, lax.rem(i, 8) // 2)

    key_row = slot_row((80, 80), 0)
    query_row = slot_row((1, 80), 1)
    query_lane = lax.broadcasted_iota(jnp.int32, (1, 80), 1)
    scale = 64 ** (-0.5)

    def group(wi, base, s):
        cols = pl.ds(pl.multiple_of(base + s * 128, 128), 128)
        own = xe[4 * wi : 4 * wi + 4, :, cols].reshape(64, 128)
        return jnp.concatenate([own, lrx[wi, :, cols]], axis=0)

    def both(x):
        return jnp.concatenate([x * mask0, x * mask1], axis=0)

    def global_row(wi, r):
        return lat * 16 - SHIFT + 4 * wi + r

    def forward(s, carry):
        attn = []
        bias = bias_ref[pl.ds(2 * s, 2)]
        for wi in range(5):
            q = group(wi, 0, s)
            kk = both(group(wi, hd, s))
            vv = both(group(wi, 2 * hd, s))
            score = (dot(kk, q, 1, 1) * scale).reshape(2, 80, 80) + bias
            if wi in (0, 4):
                rows = global_row(wi, key_row)
                score = jnp.where((rows >= 0) & (rows < nlat * 16), score, NEG)
            peak = jnp.max(score, axis=1, keepdims=True)
            expo = jnp.exp(score - peak)
            total = jnp.sum(expo, axis=1, keepdims=True)
            prob = expo / total
            if wi in (0, 4):
                rows = global_row(wi, query_row)
                keep = ((rows >= 0) & (rows < nlat * 16)).astype(F32)
                prob = prob * keep.reshape(1, 1, 80)
            prob = prob.reshape(160, 80)
            prob_ref[s, wi] = prob
            attn.append(dot(prob.astype(BF), vv, 0, 0)[0:64].astype(BF))
        attn = jnp.concatenate(attn, axis=0)[32:288]
        og = xe[2:18, :, og0:width].reshape(256, model)
        term = dot(attn, og, 0, 0).astype(BF).reshape(4, 2, 16, model)
        mb[pl.ds(4 * s, 4)] = term
        rsc(s).start()
        return carry

    def rsc(s):
        rows = pl.ds(4 * s, 4)
        return remote(
            mb.at[rows, 1 - core],
            rc.at[rows],
            rsc_s.at[s],
            rsc_r.at[s],
            at(xl, z, xh, y, 1 - core),
        )

    lax.fori_loop(0, slabs, forward, 0)

    for d, _, zsrc in zs:
        agz(d, zsrc, zsrc).wait_recv()

    def agx(a, b, xlslot, xhslot, xl_, xh_):
        return remote(
            wz,
            wf.at[pl.ds(xlslot * nz, nz), core, :, pl.ds(xhslot * half, half)],
            agx_s.at[a, b],
            agx_r.at[a, b],
            at(xl_, z, xh_, y, core),
        )

    agx_sent = [agx(a, b, xl, xh, xl ^ a, xh ^ b) for a, b in xs]
    for copy in agx_sent:
        copy.start()
    wf[pl.ds(xl * nz, nz), core, :, pl.ds(xh * half, half)] = wz[...]

    def agc(a, b):
        xl_, xh_ = xl ^ a, xh ^ b
        piece = wf.at[pl.ds(xl_ * nz, nz), core, :, pl.ds(xh_ * half, half)]
        return remote(piece, piece, agc_s.at[a, b], agc_r.at[a, b], at(xl, z, xh, y, 1 - core))

    def agc_got(a, b):
        piece = wf.at[pl.ds((xl ^ a) * nz, nz), 1 - core, :, pl.ds((xh ^ b) * half, half)]
        return remote(piece, piece, agc_s.at[a, b], agc_r.at[a, b], at(xl, z, xh, y, 1 - core))

    agc(0, 0).start()

    def core_sum(s, carry):
        rsc(s).wait_recv()
        rows = pl.ds(4 * s, 4)
        mc[rows] = (mb[rows, core].astype(F32) + rc[rows].astype(F32)).astype(BF)
        return carry

    lax.fori_loop(0, slabs, core_sum, 0)

    def rsx(a, b, slot_xl, slot_xh):
        xl_, xh_ = xl ^ a, xh ^ b
        return remote(
            mc.at[pl.ds(xl_ * nz, nz), :, pl.ds(xh_ * half, half)],
            rx.at[slot_xl * XH + slot_xh],
            rsx_s.at[a, b],
            rsx_r.at[a, b],
            at(xl_, z, xh_, y, core),
        )

    rsx_sent = [rsx(a, b, xl, xh) for a, b in xs]
    for copy in rsx_sent:
        copy.start()
    rx[xl * XH + xh] = mc[pl.ds(xl * nz, nz), :, pl.ds(xh * half, half)]

    gate_row = gate_ref[0:1, :]
    for wi in range(5):
        own = xe[4 * wi : 4 * wi + 4, :, og0:width].reshape(64, model)
        ge[wi, 0:64] = (own.astype(F32) * gate_row).astype(BF)
        ge[wi, 64:80] = (lrx[wi, :, og0:width].astype(F32) * gate_row).astype(BF)

    for a, b in xs:
        agx(a, b, xl ^ a, xh ^ b, xl ^ a, xh ^ b).wait_recv()
        agc(a, b).start()
    for a, b in [(0, 0)] + xs:
        agc_got(a, b).wait_recv()

    def backward(s, carry):
        weight = wf[pl.ds(4 * s, 4)].reshape(128, model)
        cot = dot(ge[...].reshape(400, model), weight, 1, 1).astype(BF)
        bias_sum = jnp.zeros((160, 80), F32)
        cols = pl.ds(pl.multiple_of(s * 128, 128), 128)
        for wi in range(5):
            q = group(wi, 0, s)
            kk = both(group(wi, hd, s))
            vv = both(group(wi, 2 * hd, s))
            c = cot[80 * wi : 80 * wi + 80]
            prob = prob_ref[s, wi].reshape(2, 80, 80)
            dprob = dot(vv, c, 1, 1).reshape(2, 80, 80)
            inner = jnp.sum(prob * dprob, axis=1, keepdims=True)
            dscore = (prob * (dprob - inner)).reshape(160, 80)
            if wi in (0, 4):
                first, last = (32, 64) if wi == 0 else (0, 32)
            else:
                first, last = 0, 64
            mine = (query_lane >= first) & (query_lane < last)
            bias_sum = bias_sum + jnp.where(mine, dscore, 0.0)
            ds = dscore.astype(BF)
            pb = prob.reshape(160, 80).astype(BF)
            dq = dot(ds, kk, 0, 0)[0:64] * scale
            own_ds = jnp.concatenate([ds[0:64], ds[80:144]], axis=0)
            own_pb = jnp.concatenate([pb[0:64], pb[80:144]], axis=0)
            dk = dot(own_ds, q, 1, 0) * scale
            dv = dot(own_pb, c, 1, 0)
            dk = jnp.where(low_lanes, dk[0:64], dk[64:128])
            dv = jnp.where(low_lanes, dv[0:64], dv[64:128])
            rows = slice(4 * wi, 4 * wi + 4)
            dqs[rows, :, cols] = dq.astype(BF).reshape(4, 16, 128)
            dks[rows, :, cols] = dk.astype(BF).reshape(4, 16, 128)
            dvs[rows, :, cols] = dv.astype(BF).reshape(4, 16, 128)
        high = lax.Precision.HIGHEST
        folded = dot(foldk[...], bias_sum, 1, 0, high)
        bterm[pl.ds(pl.multiple_of(32 * s, 32), 32), :] = dot(folded, foldq[...], 1, 0, high)
        return carry

    lax.fori_loop(0, slabs, backward, 0)

    outs = [
        pltpu.make_async_copy(dqs.at[2:18], dq_out.at[0], out_sem.at[0]),
        pltpu.make_async_copy(dks.at[2:18], dk_out.at[0], out_sem.at[1]),
        pltpu.make_async_copy(dvs.at[2:18], dv_out.at[0], out_sem.at[2]),
    ]
    for copy in outs:
        copy.start()

    for a, b in xs:
        rsx(a, b, xl ^ a, xh ^ b).wait_recv()
    for i in range(nz):
        total = rx[0, i].astype(F32)
        for j in range(1, XL * XH):
            total = total + rx[j, i].astype(F32)
        mz[i] = total.astype(BF)

    def rsz(d, z_, zslot):
        return remote(
            mz.at[z_], rz.at[zslot], rsz_s.at[d], rsz_r.at[d], at(xl, z_, xh, y, core)
        )

    rsz_sent = [rsz(d, z_, z) for d, z_, _ in zs]
    for copy in rsz_sent:
        copy.start()
    rz[z] = mz[z]

    term_row = lax.broadcasted_iota(jnp.int32, (16 * heads, 128), 0)
    key_place = lax.rem(term_row, 16)
    offset = lax.broadcasted_iota(jnp.int32, (16 * heads, 128), 1)
    by_offset = jnp.zeros((16 * heads, 128), F32)
    for p in range(16):
        goal = 7 * (p // 4 - key_place // 4 + 3) + (p % 4 - lax.rem(key_place, 4) + 3)
        by_offset = by_offset + jnp.where(offset == goal, bterm[:, p : p + 1], 0.0)
    by_offset = jnp.sum(by_offset.reshape(heads, 16, 128), axis=1)
    if heads < 8:
        by_offset = jnp.concatenate([by_offset, jnp.zeros((8 - heads, 128), F32)], axis=0)
    ay[y, core] = by_offset

    def ary(dy, dc, y_, core_, yslot, cslot):
        return remote(
            ay.at[yslot, cslot],
            ay.at[yslot, cslot],
            ary_s.at[dy, dc],
            ary_r.at[dy, dc],
            at(xl, z, xh, y_, core_),
        )

    ary_sent = [ary(dy, dc, y_, core_, y, core) for dy, dc, y_, _, core_ in ys]
    for copy in ary_sent:
        copy.start()

    for d, z_, zsrc in zs:
        rsz(d, zsrc, zsrc).wait_recv()
    total = rz[0].astype(F32)
    for j in range(1, nz):
        total = total + rz[j].astype(F32)
    rsum[...] = total.astype(BF)

    def rsy(dy, dc, y_, core_, yslot, cslot):
        cols = pl.ds(pl.multiple_of((y_ // 2) * 128, 128), 128)
        return remote(
            rsum.at[:, cols],
            ry.at[cslot, yslot],
            rsy_s.at[dy, dc],
            rsy_r.at[dy, dc],
            at(xl, z, xh, y_, core_),
        )

    rsy_sent = [rsy(dy, dc, y_, core_, y, core) for dy, dc, y_, _, core_ in ys]
    for copy in rsy_sent:
        copy.start()
    ry[core, y] = rsum[:, pl.ds(pl.multiple_of((y // 2) * 128, 128), 128)]

    for dy, dc, _, ysrc, csrc in ys:
        ary(dy, dc, ysrc, csrc, ysrc, csrc).wait_recv()
    bias_total = ay[0, 0] + ay[0, 1]
    for j in range(1, ny):
        bias_total = bias_total + ay[j, 0] + ay[j, 1]

    for dy, dc, _, ysrc, csrc in ys:
        rsy(dy, dc, ysrc, csrc, ysrc, csrc).wait_recv()
    block = []
    for c in range(2):
        total = ry[c, 0].astype(F32)
        for j in range(1, ny):
            total = total + ry[c, j].astype(F32)
        block.append(total)
    block = jnp.concatenate(block, axis=0)
    my_lanes = pl.ds(pl.multiple_of((lon // 4) * 128, 128), 128)
    gate_mine = gate_ref[0:1, my_lanes]
    back = lax.rem(128 - lane0, 128)
    weight_mine = wf[lat, :, :, my_lanes].reshape(32, 128).astype(F32)
    gate_term = jnp.sum(weight_mine * block, axis=0, keepdims=True)
    wg_out[...] = pltpu.roll(block * gate_mine * factor, back, 1)[:, 0:32]

    az[z, 0:8] = bias_total
    az[z, 8:16] = jnp.broadcast_to(gate_term, (8, 128))

    def arz(d, z_, zslot):
        return remote(
            az.at[zslot], az.at[zslot], arz_s.at[d], arz_r.at[d], at(xl, z_, xh, y, core)
        )

    arz_sent = [arz(d, z_, z) for d, z_, _ in zs]
    for copy in arz_sent:
        copy.start()

    emb_rows = 2 * half_emb // nlat
    index = lat * emb_rows + lax.broadcasted_iota(jnp.int32, (emb_rows, 128), 0)
    freq = lax.rem(index, half_emb).astype(F32)
    angle = tval * jnp.exp(decay * freq / half_emb)
    emb_mine = jnp.where(index < half_emb, jnp.cos(angle), jnp.sin(angle))

    for d, _, zsrc in zs:
        arz(d, zsrc, zsrc).wait_recv()
    total = az[0]
    for j in range(1, nz):
        total = total + az[j]
    ax[xl * XH + xh] = total

    def arx(a, b, slot):
        return remote(
            ax.at[slot], ax.at[slot], arx_s.at[a, b], arx_r.at[a, b], at(xl ^ a, z, xh ^ b, y, core)
        )

    arx_sent = [arx(a, b, xl * XH + xh) for a, b in xs]
    for copy in arx_sent:
        copy.start()
    for a, b in xs:
        arx(a, b, (xl ^ a) * XH + (xh ^ b)).wait_recv()
    bias_total = ax[0, 0:8] + ax[1, 0:8] + (ax[2, 0:8] + ax[3, 0:8])
    bg_out[...] = bias_total[0:heads, 0:49] * factor
    gate_sum = (ax[xh, 8:9] + ax[XH + xh, 8:9]) * factor
    gate_sum = pltpu.roll(jnp.broadcast_to(gate_sum, (8, 128)), back, 1)
    tg_out[...] = (emb_mine * gate_sum[0:1])[:, 0:32]

    for copy in outs:
        copy.wait()
    sent = agy_sent + halos + agz_sent + agx_sent + rsx_sent + rsz_sent
    sent += ary_sent + rsy_sent + arz_sent + arx_sent
    sent += [agc(a, b) for a, b in [(0, 0)] + xs]
    for copy in sent:
        copy.wait_send()
    lax.fori_loop(0, slabs, lambda s, c: (rsc(s).wait_send(), c)[1], 0)


def body(
    query_field, key_field, value_field, out_grad, out_weight, time_weight, rel_bias, timesteps
):
    frames, tile_rows, tile_cols, hd = query_field.shape
    model = out_grad.shape[3]
    heads = rel_bias.shape[0]
    nlat, nlon = lax.axis_size("lat"), lax.axis_size("lon")
    nz, ny = nlat // XL, nlon // (2 * XH)
    factor = 1.0 / math.sqrt(frames * tile_rows * nlat * tile_cols * nlon)
    half = model // XH
    slabs = hd // 128
    width = 3 * hd + model
    selq, selk = strip_tables()
    offs, foldk, foldq = place_tables()
    vmem = pl.BlockSpec(memory_space=pltpu.VMEM)
    smem = pl.BlockSpec(memory_space=pltpu.SMEM)
    hbm = pl.BlockSpec(memory_space=pl.ANY)
    dma = pltpu.SemaphoreType.DMA
    field = jax.ShapeDtypeStruct(query_field.shape, BF)
    sems = [dma((4,)), dma((3,))]
    for shape in (
        (8,),
        (ny, 2),
        (nz,),
        (XL, XH),
        (XL, XH),
        (slabs,),
        (XL, XH),
        (nz,),
        (ny, 2),
        (ny, 2),
        (nz,),
        (XL, XH),
    ):
        sems += [dma(shape), dma(shape)]
    return pl.pallas_call(
        functools.partial(kernel, nz, ny, hd, model, factor),
        out_shape=(
            field,
            field,
            field,
            jax.ShapeDtypeStruct(out_weight.shape, F32),
            jax.ShapeDtypeStruct((time_weight.shape[0] // nlat, model // nlon), F32),
            jax.ShapeDtypeStruct(rel_bias.shape, F32),
        ),
        in_specs=[hbm, hbm, hbm, hbm, vmem, vmem, smem, smem, vmem, vmem, vmem, vmem, vmem],
        out_specs=(hbm, hbm, hbm, vmem, vmem, vmem),
        scratch_shapes=[
            pltpu.VMEM((20, 16, width), BF),
            pltpu.VMEM((5, 16, width), BF),
            pltpu.VMEM((2, 7, 3, 16, hd), BF),
            pltpu.VMEM((2, 7, 3, 16, hd), BF),
            pltpu.VMEM((2, 16, 128), BF),
            pltpu.VMEM((ny, 2, 16, 128), BF),
            pltpu.VMEM((nz, 16, half), BF),
            pltpu.VMEM((nlat, 2, 16, model), BF),
            pltpu.VMEM((5, 80, model), BF),
            pltpu.VMEM((8, model), F32),
            pltpu.VMEM((heads, 80, 80), F32),
            pltpu.VMEM((slabs, 5, 160, 80), F32),
            pltpu.VMEM((nlat, 2, 16, model), BF),
            pltpu.VMEM((nlat, 16, model), BF),
            pltpu.VMEM((nlat, 16, model), BF),
            pltpu.VMEM((XL * XH, nz, 16, half), BF),
            pltpu.VMEM((nz, 16, half), BF),
            pltpu.VMEM((nz, 16, half), BF),
            pltpu.VMEM((2, ny, 16, 128), BF),
            pltpu.VMEM((16, half), BF),
            pltpu.VMEM((20, 16, hd), BF),
            pltpu.VMEM((20, 16, hd), BF),
            pltpu.VMEM((20, 16, hd), BF),
            pltpu.VMEM((16 * heads, 16), F32),
            pltpu.VMEM((ny, 2, 8, 128), F32),
            pltpu.VMEM((nz, 16, 128), F32),
            pltpu.VMEM((XL * XH, 16, 128), F32),
        ]
        + sems,
        compiler_params=pltpu.CompilerParams(
            collective_id=0, has_side_effects=True, vmem_limit_bytes=48 * 1024 * 1024
        ),
        cost_estimate=pl.CostEstimate(
            flops=2_000_000_000, bytes_accessed=4_000_000, transcendentals=1_000_000
        ),
    )(
        query_field,
        key_field,
        value_field,
        out_grad,
        out_weight,
        time_weight,
        rel_bias,
        timesteps,
        jnp.asarray(selq, BF),
        jnp.asarray(selk, BF),
        jnp.asarray(offs),
        jnp.asarray(foldk),
        jnp.asarray(foldq),
    )


def solution(mesh):
    tile = P(None, "lat", "lon", None)
    return jax.shard_map(
        body,
        mesh=mesh,
        in_specs=(tile, tile, tile, tile, P("lat", "lon"), P(), P(), P()),
        out_specs=(tile, tile, tile, P("lat", "lon"), P("lat", "lon"), P()),
        check_vma=False,
    )
```

```python
import functools
import math

import jax
import jax.numpy as jnp
import numpy as np
from jax import lax
from jax.experimental import pallas as pl
from jax.experimental.pallas import tpu as pltpu
from jax.sharding import PartitionSpec as P

SHIFT = 2
XL = 2
XH = 2
NEG = -1e9
VMEM_LIMIT = 60 * 1024 * 1024
MESH = pl.DeviceIdType.MESH
BF = jnp.bfloat16
F32 = jnp.float32


def strip_tables():
    first = np.zeros((2, 7, 16, 256), np.float32)
    second = np.zeros((2, 7, 16, 256), np.float32)
    for way, col0 in ((0, 14), (1, 0)):
        for block in range(7):
            for r in range(4):
                if block < 5:
                    row = 4 * block + r - SHIFT
                elif block == 5:
                    row = 14 + r if r < 2 else -1
                else:
                    row = r - 2 if r >= 2 else -1
                if not 0 <= row < 16:
                    continue
                for c in range(2):
                    token = row * 16 + col0 + c
                    low = r * 2 + c
                    first[way, block, low if way == 0 else low + 8, token] = 1.0
                    second[way, block, low + 8 if way == 0 else low, token] = 1.0
    return first.reshape(224, 256), second.reshape(224, 256)


def slot_places(swap):
    places = [(i // 16, i % 16 + SHIFT) for i in range(64)]
    left = [(r, c) for r in range(4) for c in range(2)]
    right = [(r, 18 + c) for r in range(4) for c in range(2)]
    return places + (right + left if swap else left + right)


def place_tables():
    queries, keys = slot_places(False), slot_places(True)
    offsets = np.full((80, 80), 49, np.int32)
    for k, (kr, kc) in enumerate(keys):
        for q, (qr, qc) in enumerate(queries):
            if kc // 4 == qc // 4:
                offsets[k, q] = 7 * (qr - kr + 3) + (qc % 4 - kc % 4 + 3)
    fold_keys = np.zeros((32, 160), np.float32)
    for head in range(2):
        for k, (kr, kc) in enumerate(keys):
            fold_keys[head * 16 + kr * 4 + kc % 4, head * 80 + k] = 1.0
    fold_queries = np.zeros((80, 16), np.float32)
    for q, (qr, qc) in enumerate(queries):
        fold_queries[q, qr * 4 + qc % 4] = 1.0
    return offsets, fold_keys, fold_queries


def dot(a, b, ca, cb, precision=None):
    return lax.dot_general(
        a, b, (((ca,), (cb,)), ((), ())), precision=precision, preferred_element_type=F32
    )


def kernel(
    nz,
    ny,
    hd,
    model,
    factor,
    q_in,
    k_in,
    v_in,
    og_in,
    w_hbm,
    tw_hbm,
    rel_hbm,
    t_hbm,
    sel_hbm,
    offs_hbm,
    foldk_hbm,
    foldq_hbm,
    dq_out,
    dk_out,
    dv_out,
    wg_hbm,
    tg_hbm,
    bg_hbm,
    w_in,
    tw_in,
    rel_in,
    t_in,
    sel,
    offs,
    foldk,
    foldq,
    xe,
    lrx,
    snd,
    rcv,
    snd2,
    rcv2,
    slab,
    slab_got,
    yb,
    wz,
    wf,
    ge,
    gate_ref,
    emb_mine,
    bias_ref,
    prob_ref,
    probb_ref,
    dscore_ref,
    cot_ref,
    mb,
    rc,
    mc,
    rx,
    mz,
    rz,
    rsum,
    ry,
    fin,
    dqs,
    dks,
    dvs,
    bterm,
    pay,
    ax,
    az,
    ay,
    wg_out,
    tg_out,
    bg_out,
    load_sem,
    out_sem,
    halo_s,
    halo_r,
    ag0_s,
    ag0_r,
    agy_s,
    agy_r,
    agz_s,
    agz_r,
    agx_s,
    agx_r,
    agc_s,
    agc_r,
    rsc_s,
    rsc_r,
    rsx_s,
    rsx_r,
    rsz_s,
    rsz_r,
    rsy_s,
    rsy_r,
    ary_s,
    ary_r,
    arz_s,
    arz_r,
    arx_s,
    arx_r,
):
    lat = lax.axis_index("lat")
    lon = lax.axis_index("lon")
    nlat, nlon = XL * nz, XH * ny * 2
    xl, z = lat // nz, lat % nz
    xh, y, core = lon // (2 * ny), (lon // 2) % ny, lon % 2
    half = model // XH
    slabs = hd // 128
    heads = hd // 64
    width = 3 * hd + model
    og0 = 3 * hd
    groups = ny // 2

    def at(xl_, z_, xh_, y_, core_):
        return (xl_ * nz + z_, xh_ * 2 * ny + y_ * 2 + core_)

    zs = [(d, lax.rem(z + d, nz), lax.rem(z - d + nz, nz)) for d in range(1, nz)]
    xs = [(a, b) for a in range(XL) for b in range(XH) if a + b]
    xcs = [(a, b, c) for a in range(XL) for b in range(XH) for c in range(2) if a + b + c]
    ys = [(d, lax.rem(y + d, ny), lax.rem(y - d + ny, ny)) for d in range(1, ny)]
    up, down = lax.rem(lat + nlat - 1, nlat), lax.rem(lat + 1, nlat)
    left, right = lax.rem(lon + nlon - 1, nlon), lax.rem(lon + 1, nlon)

    def remote(src, dst, send, recv, device):
        return pltpu.make_async_remote_copy(
            src_ref=src,
            dst_ref=dst,
            send_sem=send,
            recv_sem=recv,
            device_id=device,
            device_id_type=MESH,
        )

    barrier = pltpu.get_barrier_semaphore()
    sibling = at(xl, z, xh, y, 1 - core)
    peers = [sibling]
    peers += [at(xl, z, xh, y_, core) for _, y_, _ in ys]
    peers += [at(xl, z_, xh, y, core) for _, z_, _ in zs]
    peers += [at(xl ^ a, z, xh ^ b, y, core ^ c) for a, b, c in xcs]
    peers += [(up, lon), (down, lon)]
    peers += [(i, j) for j in (left, right) for i in (lat, up, down)]
    for peer in peers:
        pl.semaphore_signal(barrier, inc=1, device_id=peer, device_id_type=MESH)

    loads = [
        (w_hbm, w_in),
        (q_in.at[0], xe.at[2:18, :, 0:hd]),
        (k_in.at[0], xe.at[2:18, :, hd : 2 * hd]),
        (v_in.at[0], xe.at[2:18, :, 2 * hd : og0]),
        (og_in.at[0], xe.at[2:18, :, og0:width]),
        (sel_hbm, sel),
        (t_hbm, t_in),
        (tw_hbm, tw_in),
        (rel_hbm, rel_in),
        (offs_hbm, offs),
        (foldk_hbm, foldk),
        (foldq_hbm, foldq),
    ]
    loads = [pltpu.make_async_copy(a, b, load_sem.at[i]) for i, (a, b) in enumerate(loads)]
    for load in loads:
        load.start()

    lane = lax.broadcasted_iota(jnp.int32, (32, 128), 1)
    row = lax.broadcasted_iota(jnp.int32, (32, 128), 0)
    lane0 = lax.rem(lon, 4) * 32
    spread = (lane == row + lane0).astype(F32).astype(BF)
    loads[0].wait()
    slab[...] = dot(w_in[...], spread, 1, 0).astype(BF).reshape(2, 16, 128)
    pl.semaphore_wait(barrier, len(peers))
    ag0 = remote(slab.at[1 - core], slab_got, ag0_s.at[0], ag0_r.at[0], sibling)
    ag0.start()

    for load in loads[1:5]:
        load.wait()
    lat_qkv = [
        remote(
            xe.at[16:18, :, 0:og0], xe.at[0:2, :, 0:og0], halo_s.at[0], halo_r.at[0], (down, lon)
        ),
        remote(
            xe.at[2:4, :, 0:og0], xe.at[18:20, :, 0:og0], halo_s.at[1], halo_r.at[1], (up, lon)
        ),
    ]
    for copy in lat_qkv:
        copy.start()

    ag0.wait_recv()
    yb[y] = slab[core] + slab_got[...]

    def agy(d, y_, slot):
        return remote(yb.at[slot], yb.at[slot], agy_s.at[d], agy_r.at[d], at(xl, z, xh, y_, core))

    agy_sent = [agy(d, y_, y) for d, y_, _ in ys]
    for copy in agy_sent:
        copy.start()

    loads[5].wait()
    fields = [
        xe[2:18, :, 0:hd].reshape(256, hd),
        xe[2:18, :, hd : 2 * hd].reshape(256, hd),
        xe[2:18, :, og0 : og0 + half].reshape(256, hd),
        xe[2:18, :, 2 * hd : og0].reshape(256, hd),
        xe[2:18, :, og0 + half : width].reshape(256, hd),
    ]
    sq, sk = sel[0:224].astype(BF), sel[224:448].astype(BF)
    snd[:, :, 0] = (
        (dot(sq, fields[0], 1, 0) + dot(sk, fields[1], 1, 0)).astype(BF).reshape(2, 7, 16, hd)
    )
    snd[:, :, 1] = (
        (dot(sq, fields[2], 1, 0) + dot(sk, fields[3], 1, 0)).astype(BF).reshape(2, 7, 16, hd)
    )

    def strips(src, dst, base):
        devices = [
            (0, slice(0, 5), (lat, right)),
            (1, slice(0, 5), (lat, left)),
            (0, 5, (down, right)),
            (0, 6, (up, right)),
            (1, 5, (down, left)),
            (1, 6, (up, left)),
        ]
        return [
            remote(
                src.at[way, part],
                dst.at[way, part],
                halo_s.at[base + i],
                halo_r.at[base + i],
                device,
            )
            for i, (way, part, device) in enumerate(devices)
        ]

    lon_qkv = strips(snd, rcv, 2)
    for copy in lon_qkv:
        copy.start()
    snd2[...] = dot(sq, fields[4], 1, 0).astype(BF).reshape(2, 7, 16, hd)
    late = [
        remote(
            xe.at[16:18, :, og0:width],
            xe.at[0:2, :, og0:width],
            halo_s.at[8],
            halo_r.at[8],
            (down, lon),
        ),
        remote(
            xe.at[2:4, :, og0:width],
            xe.at[18:20, :, og0:width],
            halo_s.at[9],
            halo_r.at[9],
            (up, lon),
        ),
    ]
    late += strips(snd2, rcv2, 10)
    for copy in late:
        copy.start()

    for load in loads[6:]:
        load.wait()
    tval = t_in[0, 0].astype(F32)
    half_emb = tw_in.shape[0] // 2
    decay = -math.log(10000.0)
    freq = lax.broadcasted_iota(jnp.int32, (16, half_emb), 1).astype(F32)
    angle = tval * jnp.exp(decay * freq / half_emb)
    emb = jnp.concatenate([jnp.cos(angle), jnp.sin(angle)], axis=1)
    emb_hi = emb.astype(BF).astype(F32)
    emb_mid = (emb - emb_hi).astype(BF).astype(F32)
    emb_lo = emb - emb_hi - emb_mid
    emb_row = lax.broadcasted_iota(jnp.int32, (16, 2 * half_emb), 0)
    parts = jnp.where(
        emb_row == 0,
        emb_hi,
        jnp.where(emb_row == 1, emb_mid, jnp.where(emb_row == 2, emb_lo, 0.0)),
    ).astype(BF)
    gate = jnp.sum(dot(parts, tw_in[...], 1, 0), axis=0, keepdims=True)
    gate_ref[...] = jnp.broadcast_to(gate, (8, model))
    emb_rows = 2 * half_emb // nlat
    index = lat * emb_rows + lax.broadcasted_iota(jnp.int32, (emb_rows, 128), 0)
    freq = lax.rem(index, half_emb).astype(F32)
    angle = tval * jnp.exp(decay * freq / half_emb)
    emb_mine[...] = jnp.where(index < half_emb, jnp.cos(angle), jnp.sin(angle))

    def bias_rows(i, carry):
        rows = pl.ds(pl.multiple_of(i * 16, 16), 16)
        code = offs[rows, :]
        acc = [jnp.full((16, 80), NEG, F32) for _ in range(heads)]
        for o in range(49):
            hit = code == o
            acc = [jnp.where(hit, rel_in[h, o], acc[h]) for h in range(heads)]
        for h in range(heads):
            bias_ref[h, rows, :] = acc[h]
        return carry

    lax.fori_loop(0, 5, bias_rows, 0)

    for d, _, ysrc in ys:
        agy(d, ysrc, ysrc).wait_recv()
    for g in range(groups):
        wz[z, :, g * 128 : (g + 1) * 128] = yb[2 * g] + yb[2 * g + 1]

    def agz(d, z_, zslot):
        return remote(
            wz.at[zslot], wz.at[zslot], agz_s.at[d], agz_r.at[d], at(xl, z_, xh, y, core)
        )

    agz_sent = [agz(d, z_, z) for d, z_, _ in zs]
    for copy in agz_sent:
        copy.start()

    for copy in lat_qkv + lon_qkv:
        copy.wait_recv()
    top = (lax.broadcasted_iota(jnp.int32, (16, hd), 0) < 8).astype(F32).astype(BF)
    bot = (lax.broadcasted_iota(jnp.int32, (16, hd), 0) >= 8).astype(F32).astype(BF)
    for wi in range(5):
        got = []
        for m in range(2):
            pair = [rcv[0, wi, m], rcv[1, wi, m]]
            if wi == 0:
                pair = [pair[0] + rcv[0, 5, m], pair[1] + rcv[1, 5, m]]
            if wi == 4:
                pair = [pair[0] + rcv[0, 6, m], pair[1] + rcv[1, 6, m]]
            got.append(pair)
        lrx[wi, :, 0:hd] = got[0][0] * top + got[0][1] * bot
        lrx[wi, :, hd : 2 * hd] = got[0][1] * top + got[0][0] * bot
        lrx[wi, :, 2 * hd : og0] = got[1][1] * top + got[1][0] * bot
        lrx[wi, :, og0 : og0 + half] = got[1][0] * top + got[1][1] * bot

    lanes = lax.broadcasted_iota(jnp.int32, (80, 128), 1)
    mask0 = (lanes < 64).astype(F32).astype(BF)
    mask1 = (lanes >= 64).astype(F32).astype(BF)
    low_lanes = lax.broadcasted_iota(jnp.int32, (64, 128), 1) < 64

    def slot_row(shape, dim):
        i = lax.broadcasted_iota(jnp.int32, shape, dim)
        return jnp.where(i < 64, i // 16, lax.rem(i, 8) // 2)

    key_row = slot_row((80, 80), 0)
    query_row = slot_row((1, 80), 1)
    query_lane = lax.broadcasted_iota(jnp.int32, (1, 80), 1)
    scale = 64 ** (-0.5)

    def group(wi, base, s):
        cols = pl.ds(pl.multiple_of(base + s * 128, 128), 128)
        own = xe[4 * wi : 4 * wi + 4, :, cols].reshape(64, 128)
        return jnp.concatenate([own, lrx[wi, :, cols]], axis=0)

    def both(x):
        return jnp.concatenate([x * mask0, x * mask1], axis=0)

    def global_row(wi, r):
        return lat * 16 - SHIFT + 4 * wi + r

    def forward(s, carry):
        attn = []
        bias = bias_ref[pl.ds(2 * s, 2)]
        for wi in range(5):
            q = group(wi, 0, s)
            kk = both(group(wi, hd, s))
            vv = both(group(wi, 2 * hd, s))
            score = (dot(kk, q, 1, 1) * scale).reshape(2, 80, 80) + bias
            if wi in (0, 4):
                rows = global_row(wi, key_row)
                score = jnp.where((rows >= 0) & (rows < nlat * 16), score, NEG)
            peak = jnp.max(score, axis=1, keepdims=True)
            expo = jnp.exp(score - peak)
            inverse = 1.0 / jnp.sum(expo, axis=1, keepdims=True)
            if wi in (0, 4):
                rows = global_row(wi, query_row)
                keep = ((rows >= 0) & (rows < nlat * 16)).astype(F32)
                inverse = inverse * keep.reshape(1, 1, 80)
            prob = (expo * inverse).reshape(160, 80)
            prob_ref[s, wi] = prob
            prob_b = prob.astype(BF)
            probb_ref[s, wi] = prob_b
            attn.append(dot(prob_b, vv, 0, 0)[0:64].astype(BF))
        attn = jnp.concatenate(attn, axis=0)[32:288]
        og = xe[2:18, :, og0:width].reshape(256, model)
        term = dot(attn, og, 0, 0).astype(BF).reshape(4, 2, 16, model)
        mb[pl.ds(4 * s, 4)] = term
        rsc(s).start()
        return carry

    def rsc(s):
        rows = pl.ds(4 * s, 4)
        return remote(mb.at[rows, 1 - core], rc.at[rows], rsc_s.at[s], rsc_r.at[s], sibling)

    lax.fori_loop(0, slabs // 2, forward, 0)

    for d, _, zsrc in zs:
        agz(d, zsrc, zsrc).wait_recv()

    def agx(a, b, xlslot, xhslot, xl_, xh_):
        return remote(
            wz,
            wf.at[pl.ds(xlslot * nz, nz), core, :, pl.ds(xhslot * half, half)],
            agx_s.at[a, b],
            agx_r.at[a, b],
            at(xl_, z, xh_, y, core),
        )

    agx_sent = [agx(a, b, xl, xh, xl ^ a, xh ^ b) for a, b in xs]
    for copy in agx_sent:
        copy.start()
    wf[pl.ds(xl * nz, nz), core, :, pl.ds(xh * half, half)] = wz[...]

    def agc(a, b):
        xl_, xh_ = xl ^ a, xh ^ b
        piece = wf.at[pl.ds(xl_ * nz, nz), core, :, pl.ds(xh_ * half, half)]
        return remote(piece, piece, agc_s.at[a, b], agc_r.at[a, b], sibling)

    def agc_got(a, b):
        piece = wf.at[pl.ds((xl ^ a) * nz, nz), 1 - core, :, pl.ds((xh ^ b) * half, half)]
        return remote(piece, piece, agc_s.at[a, b], agc_r.at[a, b], sibling)

    agc(0, 0).start()
    lax.fori_loop(slabs // 2, slabs, forward, 0)

    def core_sum(s, carry):
        rsc(s).wait_recv()
        rows = pl.ds(4 * s, 4)
        mc[rows] = (mb[rows, core].astype(F32) + rc[rows].astype(F32)).astype(BF)
        return carry

    lax.fori_loop(0, slabs, core_sum, 0)

    def rsx(a, b, slot_xl, slot_xh):
        xl_, xh_ = xl ^ a, xh ^ b
        return remote(
            mc.at[pl.ds(xl_ * nz, nz), :, pl.ds(xh_ * half, half)],
            rx.at[slot_xl * XH + slot_xh],
            rsx_s.at[a, b],
            rsx_r.at[a, b],
            at(xl_, z, xh_, y, core),
        )

    rsx_sent = [rsx(a, b, xl, xh) for a, b in xs]
    for copy in rsx_sent:
        copy.start()
    rx[xl * XH + xh] = mc[pl.ds(xl * nz, nz), :, pl.ds(xh * half, half)]

    for copy in late:
        copy.wait_recv()
    gate_row = gate_ref[0:1, :]
    for wi in range(5):
        pair = [rcv2[0, wi], rcv2[1, wi]]
        if wi == 0:
            pair = [pair[0] + rcv2[0, 5], pair[1] + rcv2[1, 5]]
        if wi == 4:
            pair = [pair[0] + rcv2[0, 6], pair[1] + rcv2[1, 6]]
        lrx[wi, :, og0 + half : width] = pair[0] * top + pair[1] * bot
        own = xe[4 * wi : 4 * wi + 4, :, og0:width].reshape(64, model)
        ge[wi, 0:64] = (own.astype(F32) * gate_row).astype(BF)
        ge[wi, 64:80] = (lrx[wi, :, og0:width].astype(F32) * gate_row).astype(BF)

    for a, b in xs:
        agx(a, b, xl ^ a, xh ^ b, xl ^ a, xh ^ b).wait_recv()
        agc(a, b).start()
    for a, b in [(0, 0)] + xs:
        agc_got(a, b).wait_recv()

    def backward(s, gate_terms):
        weight = wf[pl.ds(4 * s, 4)].reshape(128, model)
        cot = dot(ge[...].reshape(400, model), weight, 1, 1).astype(BF)
        cot_ref[s] = cot
        bias_sum = jnp.zeros((160, 80), F32)
        for wi in range(5):
            vv = both(group(wi, 2 * hd, s))
            prob = prob_ref[s, wi].reshape(2, 80, 80)
            dprob = dot(vv, cot[80 * wi : 80 * wi + 80], 1, 1).reshape(2, 80, 80)
            inner = jnp.sum(prob * dprob, axis=1, keepdims=True)
            dscore = (prob * (dprob - inner)).reshape(160, 80)
            if wi in (0, 4):
                first, last = (32, 64) if wi == 0 else (0, 32)
            else:
                first, last = 0, 64
            mine = (query_lane >= first) & (query_lane < last)
            bias_sum = bias_sum + jnp.where(mine, dscore, 0.0)
            dscore_ref[s, wi] = dscore.astype(BF)
        folded = split_dot(foldk[...].astype(BF), bias_sum)
        bterm[pl.ds(pl.multiple_of(32 * s, 32), 32), :] = dot(
            folded, foldq[...], 1, 0, lax.Precision.HIGHEST
        )
        term = mb[pl.ds(4 * s, 4)].reshape(128, model)
        product = weight.astype(F32) * term.astype(F32)
        return gate_terms + jnp.sum(product.reshape(16, 8, model), axis=0)

    def split_dot(a, b):
        high = b.astype(BF)
        return dot(a, high, 1, 0) + dot(a, (b - high.astype(F32)).astype(BF), 1, 0)

    gate_terms = lax.fori_loop(0, slabs, backward, jnp.zeros((8, model), F32))
    gate_terms = jnp.sum(gate_terms, axis=0, keepdims=True)

    term_row = lax.broadcasted_iota(jnp.int32, (16 * heads, 128), 0)
    key_place = lax.rem(term_row, 16)
    offset = lax.broadcasted_iota(jnp.int32, (16 * heads, 128), 1)
    by_offset = jnp.zeros((16 * heads, 128), F32)
    for p in range(16):
        goal = 7 * (p // 4 - key_place // 4 + 3) + (p % 4 - lax.rem(key_place, 4) + 3)
        by_offset = by_offset + jnp.where(offset == goal, bterm[:, p : p + 1], 0.0)
    by_offset = jnp.sum(by_offset.reshape(heads, 16, 128), axis=1)
    if heads < 8:
        by_offset = jnp.concatenate([by_offset, jnp.zeros((8 - heads, 128), F32)], axis=0)
    for h in range(XH):
        pay[h, 0:8] = by_offset
        for g in range(8):
            first = h * half + min(g, groups - 1) * 128
            pay[h, 8 + g : 9 + g] = gate_terms[:, first : first + 128]

    def arx(a, b, c, slot_xl, slot_xh, slot_core, xl_, xh_, core_):
        return remote(
            pay.at[xh_],
            ax.at[slot_xl * XH + slot_xh, slot_core],
            arx_s.at[a, b, c],
            arx_r.at[a, b, c],
            at(xl_, z, xh_, y, core_),
        )

    arx_sent = [arx(a, b, c, xl, xh, core, xl ^ a, xh ^ b, core ^ c) for a, b, c in xcs]
    for copy in arx_sent:
        copy.start()
    ax[xl * XH + xh, core] = pay[xh]

    for a, b in xs:
        rsx(a, b, xl ^ a, xh ^ b).wait_recv()
    for i in range(nz):
        total = rx[0, i].astype(F32)
        for j in range(1, XL * XH):
            total = total + rx[j, i].astype(F32)
        mz[i] = total.astype(BF)

    def rsz(d, z_, zslot):
        return remote(mz.at[z_], rz.at[zslot], rsz_s.at[d], rsz_r.at[d], at(xl, z_, xh, y, core))

    rsz_sent = [rsz(d, z_, z) for d, z_, _ in zs]
    for copy in rsz_sent:
        copy.start()
    rz[z] = mz[z]

    def gradients(s, carry):
        cols = pl.ds(pl.multiple_of(s * 128, 128), 128)
        for wi in range(5):
            q = group(wi, 0, s)
            kk = both(group(wi, hd, s))
            c = cot_ref[s, 80 * wi : 80 * wi + 80]
            ds = dscore_ref[s, wi]
            pb = probb_ref[s, wi]
            dq = dot(ds, kk, 0, 0)[0:64] * scale
            own_ds = jnp.concatenate([ds[0:64], ds[80:144]], axis=0)
            own_pb = jnp.concatenate([pb[0:64], pb[80:144]], axis=0)
            dk = dot(own_ds, q, 1, 0) * scale
            dv = dot(own_pb, c, 1, 0)
            dk = jnp.where(low_lanes, dk[0:64], dk[64:128])
            dv = jnp.where(low_lanes, dv[0:64], dv[64:128])
            rows = slice(4 * wi, 4 * wi + 4)
            dqs[rows, :, cols] = dq.astype(BF).reshape(4, 16, 128)
            dks[rows, :, cols] = dk.astype(BF).reshape(4, 16, 128)
            dvs[rows, :, cols] = dv.astype(BF).reshape(4, 16, 128)
        return carry

    lax.fori_loop(0, slabs // 2, gradients, 0)

    for a, b, c in xcs:
        arx(a, b, c, xl ^ a, xh ^ b, core ^ c, xl, xh, core).wait_recv()
    total = ax[0, 0] + ax[0, 1]
    for j in range(1, XL * XH):
        total = total + (ax[j, 0] + ax[j, 1])
    az[z] = total

    def arz(d, z_, zslot):
        return remote(
            az.at[zslot], az.at[zslot], arz_s.at[d], arz_r.at[d], at(xl, z_, xh, y, core)
        )

    arz_sent = [arz(d, z_, z) for d, z_, _ in zs]
    for copy in arz_sent:
        copy.start()

    lax.fori_loop(slabs // 2, slabs, gradients, 0)
    outs = [
        pltpu.make_async_copy(dqs.at[2:18], dq_out.at[0], out_sem.at[0]),
        pltpu.make_async_copy(dks.at[2:18], dk_out.at[0], out_sem.at[1]),
        pltpu.make_async_copy(dvs.at[2:18], dv_out.at[0], out_sem.at[2]),
    ]
    for copy in outs:
        copy.start()

    for d, z_, zsrc in zs:
        rsz(d, zsrc, zsrc).wait_recv()
    total = rz[0].astype(F32)
    for j in range(1, nz):
        total = total + rz[j].astype(F32)
    rsum[...] = total.astype(BF)

    def rsy(d, y_, slot):
        cols = pl.ds(pl.multiple_of((y_ // 2) * 128, 128), 128)
        return remote(
            rsum.at[:, cols], ry.at[slot], rsy_s.at[d], rsy_r.at[d], at(xl, z, xh, y_, core)
        )

    rsy_sent = [rsy(d, y_, y) for d, y_, _ in ys]
    for copy in rsy_sent:
        copy.start()
    ry[y] = rsum[:, pl.ds(pl.multiple_of((y // 2) * 128, 128), 128)]

    for d, _, zsrc in zs:
        arz(d, zsrc, zsrc).wait_recv()
    total = az[0]
    for j in range(1, nz):
        total = total + az[j]
    ay[y] = total

    def ary(d, y_, slot):
        return remote(ay.at[slot], ay.at[slot], ary_s.at[d], ary_r.at[d], at(xl, z, xh, y_, core))

    ary_sent = [ary(d, y_, y) for d, y_, _ in ys]
    for copy in ary_sent:
        copy.start()

    for d, _, ysrc in ys:
        rsy(d, ysrc, ysrc).wait_recv()
    total = ry[0].astype(F32)
    for j in range(1, ny):
        total = total + ry[j].astype(F32)
    fin[core] = total
    swap = remote(fin.at[core], fin.at[core], ag0_s.at[1], ag0_r.at[1], sibling)
    swap_got = remote(fin.at[1 - core], fin.at[1 - core], ag0_s.at[1], ag0_r.at[1], sibling)
    swap.start()

    for d, _, ysrc in ys:
        ary(d, ysrc, ysrc).wait_recv()
    total = ay[0]
    for j in range(1, ny):
        total = total + ay[j]
    back = lax.rem(128 - lane0, 128)
    bg_out[...] = total[0:heads, 0:49] * factor
    row = lax.broadcasted_iota(jnp.int32, (8, 128), 0)
    gate_sum = jnp.sum(jnp.where(row == y // 2, total[8:16], 0.0), axis=0, keepdims=True) * factor
    gate_sum = pltpu.roll(jnp.broadcast_to(gate_sum, (8, 128)), back, 1)
    tg_out[...] = (emb_mine[...] * gate_sum[0:1])[:, 0:32]

    swap_got.wait_recv()
    gate_mine = gate_ref[0:1, pl.ds(pl.multiple_of((lon // 4) * 128, 128), 128)]
    block = fin[...].reshape(32, 128) * gate_mine * factor
    wg_out[...] = pltpu.roll(block, back, 1)[:, 0:32]
    results = [(wg_out, wg_hbm), (tg_out, tg_hbm), (bg_out, bg_hbm)]
    results = [pltpu.make_async_copy(a, b, out_sem.at[3 + i]) for i, (a, b) in enumerate(results)]
    for copy in results:
        copy.start()

    sent = [ag0, swap] + lat_qkv + lon_qkv + late + agy_sent + agz_sent + agx_sent + rsx_sent
    sent += rsz_sent + rsy_sent + ary_sent + arz_sent + arx_sent
    sent += [agc(a, b) for a, b in [(0, 0)] + xs]
    for copy in sent:
        copy.wait_send()
    lax.fori_loop(0, slabs, lambda s, c: (rsc(s).wait_send(), c)[1], 0)
    for copy in outs + results:
        copy.wait()


def body(
    query_field, key_field, value_field, out_grad, out_weight, time_weight, rel_bias, timesteps
):
    frames, tile_rows, tile_cols, hd = query_field.shape
    model = out_grad.shape[3]
    heads = rel_bias.shape[0]
    nlat, nlon = lax.axis_size("lat"), lax.axis_size("lon")
    nz, ny = nlat // XL, nlon // (2 * XH)
    factor = 1.0 / math.sqrt(frames * tile_rows * nlat * tile_cols * nlon)
    half = model // XH
    slabs = hd // 128
    width = 3 * hd + model
    selq, selk = strip_tables()
    offs, foldk, foldq = place_tables()
    hbm = pl.BlockSpec(memory_space=pltpu.HBM)
    small_outs = [
        jax.ShapeDtypeStruct(out_weight.shape, F32),
        jax.ShapeDtypeStruct((time_weight.shape[0] // nlat, model // nlon), F32),
        jax.ShapeDtypeStruct(rel_bias.shape, F32),
    ]
    dma = pltpu.SemaphoreType.DMA
    field = jax.ShapeDtypeStruct(query_field.shape, BF)
    sems = [dma((12,)), dma((6,))]
    for shape in (
        (16,),
        (2,),
        (ny,),
        (nz,),
        (XL, XH),
        (XL, XH),
        (slabs,),
        (XL, XH),
        (nz,),
        (ny,),
        (ny,),
        (nz,),
        (XL, XH, 2),
    ):
        sems += [dma(shape), dma(shape)]
    out_shape = [field, field, field] + small_outs
    results = pl.pallas_call(
        functools.partial(kernel, nz, ny, hd, model, factor),
        out_shape=out_shape,
        in_specs=[hbm] * 12,
        out_specs=[hbm] * 6,
        scratch_shapes=[
            pltpu.VMEM(out_weight.shape, BF),
            pltpu.VMEM(time_weight.shape, BF),
            pltpu.SMEM(rel_bias.shape, F32),
            pltpu.SMEM((1, 1), jnp.int32),
            pltpu.VMEM((448, 256), F32),
            pltpu.VMEM((80, 80), jnp.int32),
            pltpu.VMEM((32, 160), F32),
            pltpu.VMEM((80, 16), F32),
            pltpu.VMEM((20, 16, width), BF),
            pltpu.VMEM((5, 16, width), BF),
            pltpu.VMEM((2, 7, 2, 16, hd), BF),
            pltpu.VMEM((2, 7, 2, 16, hd), BF),
            pltpu.VMEM((2, 7, 16, hd), BF),
            pltpu.VMEM((2, 7, 16, hd), BF),
            pltpu.VMEM((2, 16, 128), BF),
            pltpu.VMEM((16, 128), BF),
            pltpu.VMEM((ny, 16, 128), BF),
            pltpu.VMEM((nz, 16, half), BF),
            pltpu.VMEM((nlat, 2, 16, model), BF),
            pltpu.VMEM((5, 80, model), BF),
            pltpu.VMEM((8, model), F32),
            pltpu.VMEM((time_weight.shape[0] // nlat, 128), F32),
            pltpu.VMEM((heads, 80, 80), F32),
            pltpu.VMEM((slabs, 5, 160, 80), F32),
            pltpu.VMEM((slabs, 5, 160, 80), BF),
            pltpu.VMEM((slabs, 5, 160, 80), BF),
            pltpu.VMEM((slabs, 400, 128), BF),
            pltpu.VMEM((nlat, 2, 16, model), BF),
            pltpu.VMEM((nlat, 16, model), BF),
            pltpu.VMEM((nlat, 16, model), BF),
            pltpu.VMEM((XL * XH, nz, 16, half), BF),
            pltpu.VMEM((nz, 16, half), BF),
            pltpu.VMEM((nz, 16, half), BF),
            pltpu.VMEM((16, half), BF),
            pltpu.VMEM((ny, 16, 128), BF),
            pltpu.VMEM((2, 16, 128), F32),
            pltpu.VMEM((20, 16, hd), BF),
            pltpu.VMEM((20, 16, hd), BF),
            pltpu.VMEM((20, 16, hd), BF),
            pltpu.VMEM((16 * heads, 16), F32),
            pltpu.VMEM((XH, 16, 128), F32),
            pltpu.VMEM((XL * XH, 2, 16, 128), F32),
            pltpu.VMEM((nz, 16, 128), F32),
            pltpu.VMEM((ny, 16, 128), F32),
        ]
        + [pltpu.VMEM(o.shape, F32) for o in small_outs]
        + sems,
        compiler_params=pltpu.CompilerParams(
            collective_id=0, has_side_effects=True, vmem_limit_bytes=VMEM_LIMIT
        ),
        cost_estimate=pl.CostEstimate(
            flops=2_000_000_000, bytes_accessed=4_000_000, transcendentals=1_000_000
        ),
    )(
        query_field,
        key_field,
        value_field,
        out_grad,
        out_weight,
        time_weight,
        rel_bias,
        timesteps.reshape(1, 1),
        jnp.asarray(np.concatenate([selq, selk])),
        jnp.asarray(offs),
        jnp.asarray(foldk),
        jnp.asarray(foldq),
    )
    return pl.pallas_call(
        hand_out,
        out_shape=out_shape,
        in_specs=[hbm] * 6,
        out_specs=[hbm] * 6,
        scratch_shapes=[pltpu.VMEM(o.shape, o.dtype) for o in out_shape] + [dma((2, 6))],
        compiler_params=pltpu.CompilerParams(vmem_limit_bytes=VMEM_LIMIT),
    )(*results)


def hand_out(*refs):
    sem = refs[18]
    loads = [pltpu.make_async_copy(refs[i], refs[12 + i], sem.at[0, i]) for i in range(6)]
    stores = [pltpu.make_async_copy(refs[12 + i], refs[6 + i], sem.at[1, i]) for i in range(6)]
    for load in loads:
        load.start()
    for load, store in zip(loads, stores):
        load.wait()
        store.start()
    for store in stores:
        store.wait()


def solution(mesh):
    tile = P(None, "lat", "lon", None)
    return jax.shard_map(
        body,
        mesh=mesh,
        in_specs=(tile, tile, tile, tile, P("lat", "lon"), P(), P(), P()),
        out_specs=(tile, tile, tile, P("lat", "lon"), P("lat", "lon"), P()),
        check_vma=False,
    )
```

```python
import functools
import math

import jax
import jax.numpy as jnp
import numpy as np
from jax import lax
from jax.experimental import pallas as pl
from jax.experimental.pallas import tpu as pltpu
from jax.sharding import PartitionSpec as P

SHIFT = 2
XL = 2
XH = 2
NEG = -1e9
VMEM_LIMIT = 60 * 1024 * 1024
MESH = pl.DeviceIdType.MESH
BF = jnp.bfloat16
F32 = jnp.float32


def strip_tables():
    first = np.zeros((2, 7, 16, 256), np.float32)
    second = np.zeros((2, 7, 16, 256), np.float32)
    for way, col0 in ((0, 14), (1, 0)):
        for block in range(7):
            for r in range(4):
                if block < 5:
                    row = 4 * block + r - SHIFT
                elif block == 5:
                    row = 14 + r if r < 2 else -1
                else:
                    row = r - 2 if r >= 2 else -1
                if not 0 <= row < 16:
                    continue
                for c in range(2):
                    token = row * 16 + col0 + c
                    low = r * 2 + c
                    first[way, block, low if way == 0 else low + 8, token] = 1.0
                    second[way, block, low + 8 if way == 0 else low, token] = 1.0
    return first.reshape(224, 256), second.reshape(224, 256)


def column_order():
    order = np.zeros((256, 256), np.float32)
    for row in range(4):
        for core in range(2):
            for j in range(32):
                order[row * 64 + core * 32 + j, core * 128 + row * 32 + j] = 1.0
    return order


def slot_places(swap):
    places = [(i // 16, i % 16 + SHIFT) for i in range(64)]
    left = [(r, c) for r in range(4) for c in range(2)]
    right = [(r, 18 + c) for r in range(4) for c in range(2)]
    return places + (right + left if swap else left + right)


def place_tables():
    queries, keys = slot_places(False), slot_places(True)
    offsets = np.full((80, 80), 49, np.int32)
    for k, (kr, kc) in enumerate(keys):
        for q, (qr, qc) in enumerate(queries):
            if kc // 4 == qc // 4:
                offsets[k, q] = 7 * (qr - kr + 3) + (qc % 4 - kc % 4 + 3)
    fold_keys = np.zeros((32, 160), np.float32)
    for head in range(2):
        for k, (kr, kc) in enumerate(keys):
            fold_keys[head * 16 + kr * 4 + kc % 4, head * 80 + k] = 1.0
    fold_queries = np.zeros((80, 16), np.float32)
    for q, (qr, qc) in enumerate(queries):
        fold_queries[q, qr * 4 + qc % 4] = 1.0
    return offsets, fold_keys, fold_queries


def dot(a, b, ca, cb, precision=None):
    return lax.dot_general(
        a, b, (((ca,), (cb,)), ((), ())), precision=precision, preferred_element_type=F32
    )


def kernel(
    nz,
    ny,
    hd,
    model,
    factor,
    q_in,
    k_in,
    v_in,
    og_in,
    w_hbm,
    tw_hbm,
    rel_hbm,
    t_hbm,
    sel_hbm,
    offs_hbm,
    foldk_hbm,
    foldq_hbm,
    dq_out,
    dk_out,
    dv_out,
    wg_hbm,
    tg_hbm,
    bg_hbm,
    w_in,
    tw_in,
    rel_in,
    t_in,
    sel,
    offs,
    foldk,
    foldq,
    xe,
    lrx,
    snd,
    rcv,
    snd2,
    rcv2,
    yb,
    wz,
    wf,
    ge,
    gate_ref,
    emb_mine,
    bias_ref,
    prob_ref,
    probb_ref,
    dscore_ref,
    cot_ref,
    mb,
    rc,
    mc,
    rx1,
    rx2,
    mz,
    rz,
    rsum,
    ry,
    dqs,
    dks,
    dvs,
    bterm,
    pay,
    ax,
    az,
    ay,
    wg_out,
    tg_out,
    bg_out,
    load_sem,
    out_sem,
    halo_s,
    halo_r,
    agy_s,
    agy_r,
    agz_s,
    agz_r,
    agx_s,
    agx_r,
    agc_s,
    agc_r,
    rsc_s,
    rsc_r,
    rsx_s,
    rsx_r,
    rsz_s,
    rsz_r,
    rsy_s,
    rsy_r,
    ary_s,
    ary_r,
    arz_s,
    arz_r,
    arx_s,
    arx_r,
):
    lat = lax.axis_index("lat")
    lon = lax.axis_index("lon")
    nlat, nlon = XL * nz, XH * ny * 2
    xl, z = lat // nz, lat % nz
    xh, y, core = lon // (2 * ny), (lon // 2) % ny, lon % 2
    half, quarter = model // 2, model // 4
    slabs = hd // 128
    heads = hd // 64
    width = 3 * hd + model
    og0 = 3 * hd
    groups = ny // 4

    def at(xl_, z_, xh_, y_, core_):
        return (xl_ * nz + z_, xh_ * 2 * ny + y_ * 2 + core_)

    far_z = sorted(range(1, nz), key=lambda d: -min(d, nz - d))
    far_y = sorted(range(1, ny), key=lambda d: -min(d, ny - d))
    zs = [(d, lax.rem(z + d, nz), lax.rem(z - d + nz, nz)) for d in far_z]
    xcs = [(a, b, c) for a in range(XL) for b in range(XH) for c in range(2) if a + b + c]
    ys = [(d, lax.rem(y + d, ny), lax.rem(y - d + ny, ny)) for d in far_y]
    up, down = lax.rem(lat + nlat - 1, nlat), lax.rem(lat + 1, nlat)
    left, right = lax.rem(lon + nlon - 1, nlon), lax.rem(lon + 1, nlon)

    def remote(src, dst, send, recv, device):
        return pltpu.make_async_remote_copy(
            src_ref=src,
            dst_ref=dst,
            send_sem=send,
            recv_sem=recv,
            device_id=device,
            device_id_type=MESH,
        )

    barrier = pltpu.get_barrier_semaphore()
    sibling = at(xl, z, xh, y, 1 - core)
    peers = [at(xl, z, xh, y_, core) for _, y_, _ in ys]
    peers += [at(xl, z_, xh, y, core) for _, z_, _ in zs]
    peers += [at(xl ^ a, z, xh ^ b, y, core ^ c) for a, b, c in xcs]
    peers += [(up, lon), (down, lon)]
    peers += [(i, j) for j in (left, right) for i in (lat, up, down)]
    peers += [sibling]
    for peer in peers:
        pl.semaphore_signal(barrier, inc=1, device_id=peer, device_id_type=MESH)

    loads = [
        (w_hbm, w_in),
        (q_in.at[0], xe.at[2:18, :, 0:hd]),
        (k_in.at[0], xe.at[2:18, :, hd : 2 * hd]),
        (v_in.at[0], xe.at[2:18, :, 2 * hd : og0]),
        (og_in.at[0], xe.at[2:18, :, og0:width]),
        (sel_hbm, sel),
        (t_hbm, t_in),
        (tw_hbm, tw_in),
        (rel_hbm, rel_in),
        (offs_hbm, offs),
        (foldk_hbm, foldk),
        (foldq_hbm, foldq),
    ]
    loads = [pltpu.make_async_copy(a, b, load_sem.at[i]) for i, (a, b) in enumerate(loads)]
    for load in loads:
        load.start()

    lane = lax.broadcasted_iota(jnp.int32, (32, 128), 1)
    row = lax.broadcasted_iota(jnp.int32, (32, 128), 0)
    lane0 = lax.rem(y, 4) * 32
    spread = (lane == row + lane0).astype(F32).astype(BF)
    loads[0].wait()
    yb[y] = dot(w_in[...], spread, 1, 0).astype(BF)
    pl.semaphore_wait(barrier, len(peers))

    def agy(d, y_, slot):
        return remote(yb.at[slot], yb.at[slot], agy_s.at[d], agy_r.at[d], at(xl, z, xh, y_, core))

    agy_sent = [agy(d, y_, y) for d, y_, _ in ys]
    for copy in agy_sent:
        copy.start()

    for load in loads[1:4]:
        load.wait()
    lat_qkv = [
        remote(
            xe.at[16:18, :, 0:og0], xe.at[0:2, :, 0:og0], halo_s.at[0], halo_r.at[0], (down, lon)
        ),
        remote(
            xe.at[2:4, :, 0:og0], xe.at[18:20, :, 0:og0], halo_s.at[1], halo_r.at[1], (up, lon)
        ),
    ]
    for copy in lat_qkv:
        copy.start()

    loads[4].wait()
    loads[5].wait()
    order = sel[448:704].astype(BF)

    def reorder(blocks):
        moved = [dot(block, order, 1, 0).astype(BF) for block in blocks]
        return [m[:, 0:128] for m in moved] + [m[:, 128:256] for m in moved]

    og_blocks = [
        xe[2:18, :, og0 + 256 * i : og0 + 256 * (i + 1)].reshape(256, 256)
        for i in range(model // 256)
    ]
    for i, block in enumerate(reorder(og_blocks)):
        xe[2:18, :, og0 + 128 * i : og0 + 128 * (i + 1)] = block.reshape(16, 16, 128)

    fields = [
        xe[2:18, :, 0:hd].reshape(256, hd),
        xe[2:18, :, hd : 2 * hd].reshape(256, hd),
        xe[2:18, :, og0 : og0 + half].reshape(256, hd),
        xe[2:18, :, 2 * hd : og0].reshape(256, hd),
        xe[2:18, :, og0 + half : width].reshape(256, hd),
    ]
    sq, sk = sel[0:224].astype(BF), sel[224:448].astype(BF)
    snd[:, :, 0] = (
        (dot(sq, fields[0], 1, 0) + dot(sk, fields[1], 1, 0)).astype(BF).reshape(2, 7, 16, hd)
    )
    snd[:, :, 1] = (
        (dot(sq, fields[2], 1, 0) + dot(sk, fields[3], 1, 0)).astype(BF).reshape(2, 7, 16, hd)
    )

    def strips(src, dst, base):
        devices = [
            (0, slice(0, 5), (lat, right)),
            (1, slice(0, 5), (lat, left)),
            (0, 5, (down, right)),
            (0, 6, (up, right)),
            (1, 5, (down, left)),
            (1, 6, (up, left)),
        ]
        return [
            remote(
                src.at[way, part],
                dst.at[way, part],
                halo_s.at[base + i],
                halo_r.at[base + i],
                device,
            )
            for i, (way, part, device) in enumerate(devices)
        ]

    lon_qkv = strips(snd, rcv, 2)
    for copy in lon_qkv:
        copy.start()

    snd2[...] = dot(sq, fields[4], 1, 0).astype(BF).reshape(2, 7, 16, hd)
    late = [
        remote(
            xe.at[16:18, :, og0:width],
            xe.at[0:2, :, og0:width],
            halo_s.at[8],
            halo_r.at[8],
            (down, lon),
        ),
        remote(
            xe.at[2:4, :, og0:width],
            xe.at[18:20, :, og0:width],
            halo_s.at[9],
            halo_r.at[9],
            (up, lon),
        ),
    ]
    late += strips(snd2, rcv2, 10)
    for copy in late:
        copy.start()

    for load in loads[6:]:
        load.wait()
    tval = t_in[0, 0].astype(F32)
    half_emb = tw_in.shape[0] // 2
    decay = -math.log(10000.0)
    freq = lax.broadcasted_iota(jnp.int32, (16, half_emb), 1).astype(F32)
    angle = tval * jnp.exp(decay * freq / half_emb)
    emb = jnp.concatenate([jnp.cos(angle), jnp.sin(angle)], axis=1)
    emb_hi = emb.astype(BF).astype(F32)
    emb_mid = (emb - emb_hi).astype(BF).astype(F32)
    emb_lo = emb - emb_hi - emb_mid
    emb_row = lax.broadcasted_iota(jnp.int32, (16, 2 * half_emb), 0)
    parts = jnp.where(
        emb_row == 0,
        emb_hi,
        jnp.where(emb_row == 1, emb_mid, jnp.where(emb_row == 2, emb_lo, 0.0)),
    ).astype(BF)
    tw_blocks = [tw_in[:, 256 * i : 256 * (i + 1)] for i in range(model // 256)]
    tw = jnp.concatenate(reorder(tw_blocks), axis=1)
    gate = jnp.sum(dot(parts, tw, 1, 0), axis=0, keepdims=True)
    gate_ref[...] = jnp.broadcast_to(gate, (8, model))
    emb_rows = 2 * half_emb // nlat
    index = lat * emb_rows + lax.broadcasted_iota(jnp.int32, (emb_rows, 128), 0)
    freq = lax.rem(index, half_emb).astype(F32)
    angle = tval * jnp.exp(decay * freq / half_emb)
    emb_mine[...] = jnp.where(index < half_emb, jnp.cos(angle), jnp.sin(angle))

    def bias_rows(i, carry):
        rows = pl.ds(pl.multiple_of(i * 16, 16), 16)
        code = offs[rows, :]
        acc = [jnp.full((16, 80), NEG, F32) for _ in range(heads)]
        for o in range(49):
            hit = code == o
            acc = [jnp.where(hit, rel_in[h, o], acc[h]) for h in range(heads)]
        for h in range(heads):
            bias_ref[h, rows, :] = acc[h]
        return carry

    lax.fori_loop(0, 5, bias_rows, 0)

    for d, _, ysrc in ys:
        agy(d, ysrc, ysrc).wait_recv()
    for g in range(groups):
        pair = [yb[4 * g + i] + yb[4 * g + i + 1] for i in (0, 2)]
        wz[z, :, g * 128 : (g + 1) * 128] = pair[0] + pair[1]

    def agz(d, z_, zslot):
        return remote(
            wz.at[zslot], wz.at[zslot], agz_s.at[d], agz_r.at[d], at(xl, z_, xh, y, core)
        )

    agz_sent = [agz(d, z_, z) for d, z_, _ in zs]
    for copy in agz_sent:
        copy.start()

    for copy in lat_qkv + lon_qkv:
        copy.wait_recv()
    top = (lax.broadcasted_iota(jnp.int32, (16, hd), 0) < 8).astype(F32).astype(BF)
    bot = (lax.broadcasted_iota(jnp.int32, (16, hd), 0) >= 8).astype(F32).astype(BF)
    for wi in range(5):
        got = []
        for m in range(2):
            pair = [rcv[0, wi, m], rcv[1, wi, m]]
            if wi == 0:
                pair = [pair[0] + rcv[0, 5, m], pair[1] + rcv[1, 5, m]]
            if wi == 4:
                pair = [pair[0] + rcv[0, 6, m], pair[1] + rcv[1, 6, m]]
            got.append(pair)
        lrx[wi, :, 0:hd] = got[0][0] * top + got[0][1] * bot
        lrx[wi, :, hd : 2 * hd] = got[0][1] * top + got[0][0] * bot
        lrx[wi, :, 2 * hd : og0] = got[1][1] * top + got[1][0] * bot
        lrx[wi, :, og0 : og0 + half] = got[1][0] * top + got[1][1] * bot

    lanes = lax.broadcasted_iota(jnp.int32, (80, 128), 1)
    mask0 = (lanes < 64).astype(F32).astype(BF)
    mask1 = (lanes >= 64).astype(F32).astype(BF)
    low_lanes = lax.broadcasted_iota(jnp.int32, (64, 128), 1) < 64

    def slot_row(shape, dim):
        i = lax.broadcasted_iota(jnp.int32, shape, dim)
        return jnp.where(i < 64, i // 16, lax.rem(i, 8) // 2)

    key_row = slot_row((80, 80), 0)
    query_row = slot_row((1, 80), 1)
    query_lane = lax.broadcasted_iota(jnp.int32, (1, 80), 1)
    scale = 64 ** (-0.5)

    def group(wi, base, s):
        cols = pl.ds(pl.multiple_of(base + s * 128, 128), 128)
        own = xe[4 * wi : 4 * wi + 4, :, cols].reshape(64, 128)
        return jnp.concatenate([own, lrx[wi, :, cols]], axis=0)

    def both(x):
        return jnp.concatenate([x * mask0, x * mask1], axis=0)

    def global_row(wi, r):
        return lat * 16 - SHIFT + 4 * wi + r

    def forward(s, carry):
        attn = []
        bias = bias_ref[pl.ds(2 * s, 2)]
        for wi in range(5):
            q = group(wi, 0, s)
            kk = both(group(wi, hd, s))
            vv = both(group(wi, 2 * hd, s))
            score = (dot(kk, q, 1, 1) * scale).reshape(2, 80, 80) + bias
            if wi in (0, 4):
                rows = global_row(wi, key_row)
                score = jnp.where((rows >= 0) & (rows < nlat * 16), score, NEG)
            peak = jnp.max(score, axis=1, keepdims=True)
            expo = jnp.exp(score - peak)
            inverse = 1.0 / jnp.sum(expo, axis=1, keepdims=True)
            if wi in (0, 4):
                rows = global_row(wi, query_row)
                keep = ((rows >= 0) & (rows < nlat * 16)).astype(F32)
                inverse = inverse * keep.reshape(1, 1, 80)
            prob = (expo * inverse).reshape(160, 80)
            prob_ref[s, wi] = prob
            prob_b = prob.astype(BF)
            probb_ref[s, wi] = prob_b
            attn.append(dot(prob_b, vv, 0, 0)[0:64].astype(BF))
        attn = jnp.concatenate(attn, axis=0)[32:288]
        og = xe[2:18, :, og0:width].reshape(256, model)
        term = dot(attn, og, 0, 0).astype(BF).reshape(4, 32, model)
        mb[pl.ds(4 * s, 4)] = term
        rsc(s).start()
        return carry

    def rsc(s):
        rows = pl.ds(4 * s, 4)
        cols = pl.ds(pl.multiple_of((1 - core) * half, 128), half)
        return remote(mb.at[rows, :, cols], rc.at[rows], rsc_s.at[s], rsc_r.at[s], sibling)

    ours, theirs = xl * (slabs // 2), (1 - xl) * (slabs // 2)
    forward(ours, 0)
    for i in range(1, slabs // 2):
        forward(ours + i, 0)

    for d, _, zsrc in zs:
        agz(d, zsrc, zsrc).wait_recv()
    near = [(1, 0), (1, 1)]

    def piece(xl_, xh_, core_, part=None):
        first, count = (xl_ * nz, nz) if part is None else (xl_ * nz + part * (nz // 2), nz // 2)
        return wf.at[pl.ds(first, count), :, pl.ds(core_ * half + xh_ * quarter, quarter)]

    def neighbour(b):
        return at(1 - xl, z, xh ^ b, y, core)

    def agx(b, part, slot_xl, slot_xh):
        rows = pl.ds(part * (nz // 2), nz // 2)
        return remote(
            wz.at[rows],
            piece(slot_xl, slot_xh, core, part),
            agx_s.at[part, b],
            agx_r.at[part, b],
            neighbour(b),
        )

    agx_sent = [agx(b, 1 - b, xl, xh) for _, b in near]
    agx_sent += [agx(b, b, xl, xh) for _, b in near]
    for copy in agx_sent:
        copy.start()
    my_cols = pl.ds(pl.multiple_of(core * half + xh * quarter, 128), quarter)
    wf[pl.ds(xl * nz, nz), :, my_cols] = wz[...]

    def agc(i, xl_, xh_, core_, part=None):
        block = piece(xl_, xh_, core_, part)
        return remote(block, block, agc_s.at[i], agc_r.at[i], sibling)

    agc_sent = [agc(0, xl, xh, core)]
    agc_sent[0].start()

    def core_sum(s):
        rsc(s).wait_recv()
        rows = pl.ds(4 * s, 4)
        cols = pl.ds(pl.multiple_of(core * half, 128), half)
        mc[rows] = (mb[rows, :, cols].astype(F32) + rc[rows].astype(F32)).astype(BF)

    def rsx1(b, part, xl_, xh_):
        rows = pl.ds(xl_ * nz + part * (nz // 2), nz // 2)
        return remote(
            mc.at[rows, :, pl.ds(pl.multiple_of(xh_ * quarter, 128), quarter)],
            rx1.at[b],
            rsx_s.at[0, b],
            rsx_r.at[0, b],
            neighbour(b),
        )

    def rsx2(b):
        return remote(
            mc.at[pl.ds((1 - xl) * nz, nz), :, pl.ds((xh ^ b) * quarter, quarter)],
            rx2.at[b],
            rsx_s.at[1, b],
            rsx_r.at[1, b],
            neighbour(b),
        )

    forward(theirs, 0)
    for i in range(slabs // 2):
        core_sum(ours + i)
    rsx_sent = [rsx1(b, b, xl, 1 - xh) for _, b in near]
    for copy in rsx_sent:
        copy.start()
    for i in range(1, slabs // 2):
        forward(theirs + i, 0)

    def relay(b, xl_, xh_):
        block = piece(xl_, xh_, core, b)
        return remote(block, block, agx_s.at[2, b], agx_r.at[2, b], neighbour(b))

    for _, b in near:
        agx(b, 1 - b, 1 - xl, xh ^ b).wait_recv()
    relays = [relay(b, 1 - xl, xh ^ b ^ 1) for _, b in near]
    for copy in relays:
        copy.start()
    for i in range(slabs // 2):
        core_sum(theirs + i)

    for copy in late:
        copy.wait_recv()
    gate_row = gate_ref[0:1, :]
    for wi in range(5):
        pair = [rcv2[0, wi], rcv2[1, wi]]
        if wi == 0:
            pair = [pair[0] + rcv2[0, 5], pair[1] + rcv2[1, 5]]
        if wi == 4:
            pair = [pair[0] + rcv2[0, 6], pair[1] + rcv2[1, 6]]
        lrx[wi, :, og0 + half : width] = pair[0] * top + pair[1] * bot
        own = xe[4 * wi : 4 * wi + 4, :, og0:width].reshape(64, model)
        ge[wi, 0:64] = (own.astype(F32) * gate_row).astype(BF)
        ge[wi, 64:80] = (lrx[wi, :, og0:width].astype(F32) * gate_row).astype(BF)

    for _, b in near:
        agx(b, b, 1 - xl, xh ^ b).wait_recv()
        agc_sent.append(agc(1 + b, 1 - xl, xh ^ b, core))
        agc_sent[-1].start()

    def backward(s, gate_terms):
        weight = wf[pl.ds(4 * s, 4)].reshape(128, model)
        cot = dot(ge[...].reshape(400, model), weight, 1, 1).astype(BF)
        cot_ref[s] = cot
        bias_sum = jnp.zeros((160, 80), F32)
        for wi in range(5):
            vv = both(group(wi, 2 * hd, s))
            prob = prob_ref[s, wi].reshape(2, 80, 80)
            dprob = dot(vv, cot[80 * wi : 80 * wi + 80], 1, 1).reshape(2, 80, 80)
            inner = jnp.sum(prob * dprob, axis=1, keepdims=True)
            dscore = (prob * (dprob - inner)).reshape(160, 80)
            if wi in (0, 4):
                first, last = (32, 64) if wi == 0 else (0, 32)
            else:
                first, last = 0, 64
            mine = (query_lane >= first) & (query_lane < last)
            bias_sum = bias_sum + jnp.where(mine, dscore, 0.0)
            dscore_ref[s, wi] = dscore.astype(BF)
        folded = split_dot(foldk[...].astype(BF), bias_sum)
        bterm[pl.ds(pl.multiple_of(32 * s, 32), 32), :] = dot(
            folded, foldq[...], 1, 0, lax.Precision.HIGHEST
        )
        term = mb[pl.ds(4 * s, 4)].reshape(128, model)
        product = weight.astype(F32) * term.astype(F32)
        return gate_terms + jnp.sum(product.reshape(16, 8, model), axis=0)

    def split_dot(a, b):
        high = b.astype(BF)
        return dot(a, high, 1, 0) + dot(a, (b - high.astype(F32)).astype(BF), 1, 0)

    for _, b in near:
        agc(1 + b, 1 - xl, xh ^ b, 1 - core).wait_recv()
    gate_terms = backward(theirs, jnp.zeros((8, model), F32))

    for _, b in near:
        relay(b, xl, 1 - xh).wait_recv()
        agc_sent.append(agc(3 + b, xl, 1 - xh, core, b))
        agc_sent[-1].start()

    for _, b in near:
        rsx1(b, b, xl, 1 - xh).wait_recv()
        rows = pl.ds((1 - xl) * nz + b * (nz // 2), nz // 2)
        cols = pl.ds(pl.multiple_of((xh ^ b ^ 1) * quarter, 128), quarter)
        mc[rows, :, cols] = (mc[rows, :, cols].astype(F32) + rx1[b].astype(F32)).astype(BF)
    second = [rsx2(b) for _, b in near]
    for copy in second:
        copy.start()
    rsx_sent += second

    for i in range(1, slabs // 2):
        gate_terms = backward(theirs + i, gate_terms)
    agc(0, xl, xh, 1 - core).wait_recv()
    for _, b in near:
        agc(3 + b, xl, 1 - xh, 1 - core, b).wait_recv()
    gate_terms = lax.fori_loop(ours, ours + slabs // 2, backward, gate_terms)
    gate_terms = jnp.sum(gate_terms, axis=0, keepdims=True)

    term_row = lax.broadcasted_iota(jnp.int32, (16 * heads, 128), 0)
    key_place = lax.rem(term_row, 16)
    offset = lax.broadcasted_iota(jnp.int32, (16 * heads, 128), 1)
    by_offset = jnp.zeros((16 * heads, 128), F32)
    for p in range(16):
        goal = 7 * (p // 4 - key_place // 4 + 3) + (p % 4 - lax.rem(key_place, 4) + 3)
        by_offset = by_offset + jnp.where(offset == goal, bterm[:, p : p + 1], 0.0)
    by_offset = jnp.sum(by_offset.reshape(heads, 16, 128), axis=1)
    if heads < 8:
        by_offset = jnp.concatenate([by_offset, jnp.zeros((8 - heads, 128), F32)], axis=0)
    row = lax.broadcasted_iota(jnp.int32, (8, 128), 0)
    upper = lax.broadcasted_iota(jnp.int32, (8, 128), 1) >= 64
    for c in range(2):
        for h in range(XH):
            packed = by_offset
            for i in range(quarter // 64):
                first = c * half + h * quarter + (i // 2) * 128
                lanes_i = jnp.broadcast_to(gate_terms[:, first : first + 128], (8, 128))
                if i % 2 == 0:
                    lanes_i = pltpu.roll(lanes_i, 64, 1)
                packed = jnp.where(upper & (row == i), lanes_i, packed)
            pay[c, h] = packed

    def arx(a, b, c, slot_xl, slot_xh, slot_core, xl_, xh_, core_):
        return remote(
            pay.at[core_, xh_],
            ax.at[slot_xl * XH + slot_xh, slot_core],
            arx_s.at[a, b, c],
            arx_r.at[a, b, c],
            at(xl_, z, xh_, y, core_),
        )

    arx_sent = [arx(a, b, c, xl, xh, core, xl ^ a, xh ^ b, core ^ c) for a, b, c in xcs]
    for copy in arx_sent:
        copy.start()
    ax[xl * XH + xh, core] = pay[core, xh]

    for _, b in near:
        rsx2(b).wait_recv()
    for i in range(nz):
        total = mc[xl * nz + i, :, pl.ds(pl.multiple_of(xh * quarter, 128), quarter)].astype(F32)
        mz[i] = (total + rx2[0, i].astype(F32) + rx2[1, i].astype(F32)).astype(BF)

    def rsz(d, z_, zslot):
        return remote(mz.at[z_], rz.at[zslot], rsz_s.at[d], rsz_r.at[d], at(xl, z_, xh, y, core))

    rsz_sent = [rsz(d, z_, z) for d, z_, _ in zs]
    for copy in rsz_sent:
        copy.start()
    rz[z] = mz[z]

    def gradients(s, carry):
        cols = pl.ds(pl.multiple_of(s * 128, 128), 128)
        for wi in range(5):
            q = group(wi, 0, s)
            kk = both(group(wi, hd, s))
            c = cot_ref[s, 80 * wi : 80 * wi + 80]
            ds = dscore_ref[s, wi]
            pb = probb_ref[s, wi]
            dq = dot(ds, kk, 0, 0)[0:64] * scale
            own_ds = jnp.concatenate([ds[0:64], ds[80:144]], axis=0)
            own_pb = jnp.concatenate([pb[0:64], pb[80:144]], axis=0)
            dk = dot(own_ds, q, 1, 0) * scale
            dv = dot(own_pb, c, 1, 0)
            dk = jnp.where(low_lanes, dk[0:64], dk[64:128])
            dv = jnp.where(low_lanes, dv[0:64], dv[64:128])
            rows = slice(4 * wi, 4 * wi + 4)
            dqs[rows, :, cols] = dq.astype(BF).reshape(4, 16, 128)
            dks[rows, :, cols] = dk.astype(BF).reshape(4, 16, 128)
            dvs[rows, :, cols] = dv.astype(BF).reshape(4, 16, 128)
        return carry

    lax.fori_loop(0, slabs // 2, gradients, 0)

    for a, b, c in xcs:
        arx(a, b, c, xl ^ a, xh ^ b, core ^ c, xl, xh, core).wait_recv()
    total = ax[0, 0] + ax[0, 1]
    for j in range(1, XL * XH):
        total = total + (ax[j, 0] + ax[j, 1])
    az[z] = total

    def arz(d, z_, zslot):
        return remote(
            az.at[zslot], az.at[zslot], arz_s.at[d], arz_r.at[d], at(xl, z_, xh, y, core)
        )

    arz_sent = [arz(d, z_, z) for d, z_, _ in zs]
    for copy in arz_sent:
        copy.start()

    lax.fori_loop(slabs // 2, slabs, gradients, 0)
    outs = [
        pltpu.make_async_copy(dqs.at[2:18], dq_out.at[0], out_sem.at[0]),
        pltpu.make_async_copy(dks.at[2:18], dk_out.at[0], out_sem.at[1]),
        pltpu.make_async_copy(dvs.at[2:18], dv_out.at[0], out_sem.at[2]),
    ]
    for copy in outs:
        copy.start()

    for d, z_, zsrc in zs:
        rsz(d, zsrc, zsrc).wait_recv()
    total = rz[0].astype(F32)
    for j in range(1, nz):
        total = total + rz[j].astype(F32)
    rsum[...] = total.astype(BF)

    def rsy(d, y_, slot):
        cols = pl.ds(pl.multiple_of((y_ // 4) * 128, 128), 128)
        return remote(
            rsum.at[:, cols], ry.at[slot], rsy_s.at[d], rsy_r.at[d], at(xl, z, xh, y_, core)
        )

    rsy_sent = [rsy(d, y_, y) for d, y_, _ in ys]
    for copy in rsy_sent:
        copy.start()
    ry[y] = rsum[:, pl.ds(pl.multiple_of((y // 4) * 128, 128), 128)]

    for d, _, zsrc in zs:
        arz(d, zsrc, zsrc).wait_recv()
    total = az[0]
    for j in range(1, nz):
        total = total + az[j]
    ay[y] = total

    def ary(d, y_, slot):
        return remote(ay.at[slot], ay.at[slot], ary_s.at[d], ary_r.at[d], at(xl, z, xh, y_, core))

    ary_sent = [ary(d, y_, y) for d, y_, _ in ys]
    for copy in ary_sent:
        copy.start()

    for d, _, ysrc in ys:
        rsy(d, ysrc, ysrc).wait_recv()
    total = ry[0].astype(F32)
    for j in range(1, ny):
        total = total + ry[j].astype(F32)
    back = lax.rem(128 - lane0, 128)
    first = core * half + xh * quarter + (y // 4) * 128
    gate_mine = gate_ref[0:1, pl.ds(pl.multiple_of(first, 128), 128)]
    wg_out[...] = pltpu.roll(total * gate_mine * factor, back, 1)[:, 0:32]

    for d, _, ysrc in ys:
        ary(d, ysrc, ysrc).wait_recv()
    total = ay[0]
    for j in range(1, ny):
        total = total + ay[j]
    bg_out[...] = total[0:heads, 0:49] * factor
    gate_sum = jnp.sum(jnp.where(row == y // 2, total, 0.0), axis=0, keepdims=True) * factor
    gate_sum = pltpu.roll(jnp.broadcast_to(gate_sum, (8, 128)), 64 - lax.rem(y, 2) * 32, 1)
    tg_out[...] = (emb_mine[...] * gate_sum[0:1])[:, 0:32]

    results = [(wg_out, wg_hbm), (tg_out, tg_hbm), (bg_out, bg_hbm)]
    results = [pltpu.make_async_copy(a, b, out_sem.at[3 + i]) for i, (a, b) in enumerate(results)]
    for copy in results:
        copy.start()

    sent = lat_qkv + lon_qkv + late + agy_sent + agz_sent + agx_sent + rsx_sent
    sent += rsz_sent + rsy_sent + ary_sent + arz_sent + arx_sent
    sent += relays + agc_sent
    for copy in sent:
        copy.wait_send()
    lax.fori_loop(0, slabs, lambda s, c: (rsc(s).wait_send(), c)[1], 0)
    for copy in outs + results:
        copy.wait()


def body(
    query_field, key_field, value_field, out_grad, out_weight, time_weight, rel_bias, timesteps
):
    frames, tile_rows, tile_cols, hd = query_field.shape
    model = out_grad.shape[3]
    heads = rel_bias.shape[0]
    nlat, nlon = lax.axis_size("lat"), lax.axis_size("lon")
    nz, ny = nlat // XL, nlon // (2 * XH)
    factor = 1.0 / math.sqrt(frames * tile_rows * nlat * tile_cols * nlon)
    half, quarter = model // 2, model // 4
    slabs = hd // 128
    width = 3 * hd + model
    selq, selk = strip_tables()
    order = column_order()
    offs, foldk, foldq = place_tables()
    hbm = pl.BlockSpec(memory_space=pltpu.HBM)
    small_outs = [
        jax.ShapeDtypeStruct(out_weight.shape, F32),
        jax.ShapeDtypeStruct((time_weight.shape[0] // nlat, model // nlon), F32),
        jax.ShapeDtypeStruct(rel_bias.shape, F32),
    ]
    dma = pltpu.SemaphoreType.DMA
    field = jax.ShapeDtypeStruct(query_field.shape, BF)
    sems = [dma((12,)), dma((6,))]
    for shape in (
        (16,),
        (ny,),
        (nz,),
        (3, 2),
        (5,),
        (slabs,),
        (2, 2),
        (nz,),
        (ny,),
        (ny,),
        (nz,),
        (XL, XH, 2),
    ):
        sems += [dma(shape), dma(shape)]
    out_shape = [field, field, field] + small_outs
    results = pl.pallas_call(
        functools.partial(kernel, nz, ny, hd, model, factor),
        out_shape=out_shape,
        in_specs=[hbm] * 12,
        out_specs=[hbm] * 6,
        scratch_shapes=[
            pltpu.VMEM(out_weight.shape, BF),
            pltpu.VMEM(time_weight.shape, BF),
            pltpu.SMEM(rel_bias.shape, F32),
            pltpu.SMEM((1, 1), jnp.int32),
            pltpu.VMEM((704, 256), F32),
            pltpu.VMEM((80, 80), jnp.int32),
            pltpu.VMEM((32, 160), F32),
            pltpu.VMEM((80, 16), F32),
            pltpu.VMEM((20, 16, width), BF),
            pltpu.VMEM((5, 16, width), BF),
            pltpu.VMEM((2, 7, 2, 16, hd), BF),
            pltpu.VMEM((2, 7, 2, 16, hd), BF),
            pltpu.VMEM((2, 7, 16, hd), BF),
            pltpu.VMEM((2, 7, 16, hd), BF),
            pltpu.VMEM((ny, 32, 128), BF),
            pltpu.VMEM((nz, 32, quarter), BF),
            pltpu.VMEM((nlat, 32, model), BF),
            pltpu.VMEM((5, 80, model), BF),
            pltpu.VMEM((8, model), F32),
            pltpu.VMEM((time_weight.shape[0] // nlat, 128), F32),
            pltpu.VMEM((heads, 80, 80), F32),
            pltpu.VMEM((slabs, 5, 160, 80), F32),
            pltpu.VMEM((slabs, 5, 160, 80), BF),
            pltpu.VMEM((slabs, 5, 160, 80), BF),
            pltpu.VMEM((slabs, 400, 128), BF),
            pltpu.VMEM((nlat, 32, model), BF),
            pltpu.VMEM((nlat, 32, half), BF),
            pltpu.VMEM((nlat, 32, half), BF),
            pltpu.VMEM((2, nz // 2, 32, quarter), BF),
            pltpu.VMEM((2, nz, 32, quarter), BF),
            pltpu.VMEM((nz, 32, quarter), BF),
            pltpu.VMEM((nz, 32, quarter), BF),
            pltpu.VMEM((32, quarter), BF),
            pltpu.VMEM((ny, 32, 128), BF),
            pltpu.VMEM((20, 16, hd), BF),
            pltpu.VMEM((20, 16, hd), BF),
            pltpu.VMEM((20, 16, hd), BF),
            pltpu.VMEM((16 * heads, 16), F32),
            pltpu.VMEM((2, XH, 8, 128), F32),
            pltpu.VMEM((XL * XH, 2, 8, 128), F32),
            pltpu.VMEM((nz, 8, 128), F32),
            pltpu.VMEM((ny, 8, 128), F32),
        ]
        + [pltpu.VMEM(o.shape, F32) for o in small_outs]
        + sems,
        compiler_params=pltpu.CompilerParams(
            collective_id=0, has_side_effects=True, vmem_limit_bytes=VMEM_LIMIT
        ),
        cost_estimate=pl.CostEstimate(
            flops=2_000_000_000, bytes_accessed=4_000_000, transcendentals=1_000_000
        ),
    )(
        query_field,
        key_field,
        value_field,
        out_grad,
        out_weight,
        time_weight,
        rel_bias,
        timesteps.reshape(1, 1),
        jnp.asarray(np.concatenate([selq, selk, order])),
        jnp.asarray(offs),
        jnp.asarray(foldk),
        jnp.asarray(foldq),
    )
    return pl.pallas_call(
        hand_out,
        out_shape=out_shape,
        in_specs=[hbm] * 6,
        out_specs=[hbm] * 6,
        scratch_shapes=[pltpu.VMEM(o.shape, o.dtype) for o in out_shape] + [dma((2, 6))],
        compiler_params=pltpu.CompilerParams(vmem_limit_bytes=VMEM_LIMIT),
    )(*results)


def hand_out(*refs):
    sem = refs[18]
    loads = [pltpu.make_async_copy(refs[i], refs[12 + i], sem.at[0, i]) for i in range(6)]
    stores = [pltpu.make_async_copy(refs[12 + i], refs[6 + i], sem.at[1, i]) for i in range(6)]
    for load in loads:
        load.start()
    for load, store in zip(loads, stores):
        load.wait()
        store.start()
    for store in stores:
        store.wait()


def solution(mesh):
    tile = P(None, "lat", "lon", None)
    return jax.shard_map(
        body,
        mesh=mesh,
        in_specs=(tile, tile, tile, tile, P("lat", "lon"), P(), P(), P()),
        out_specs=(tile, tile, tile, P("lat", "lon"), P("lat", "lon"), P()),
        check_vma=False,
    )
```

```python
import functools
import math

import jax
import jax.numpy as jnp
import numpy as np
from jax import lax
from jax.experimental import pallas as pl
from jax.experimental.pallas import tpu as pltpu
from jax.sharding import PartitionSpec as P

SHIFT = 2
XL = 2
XH = 2
NEG = -1e9
VMEM_LIMIT = 60 * 1024 * 1024
MESH = pl.DeviceIdType.MESH
BF = jnp.bfloat16
F32 = jnp.float32


def strip_tables():
    first = np.zeros((2, 7, 16, 256), np.float32)
    second = np.zeros((2, 7, 16, 256), np.float32)
    for way, col0 in ((0, 14), (1, 0)):
        for block in range(7):
            for r in range(4):
                if block < 5:
                    row = 4 * block + r - SHIFT
                elif block == 5:
                    row = 14 + r if r < 2 else -1
                else:
                    row = r - 2 if r >= 2 else -1
                if not 0 <= row < 16:
                    continue
                for c in range(2):
                    token = row * 16 + col0 + c
                    low = r * 2 + c
                    first[way, block, low if way == 0 else low + 8, token] = 1.0
                    second[way, block, low + 8 if way == 0 else low, token] = 1.0
    return first.reshape(224, 256), second.reshape(224, 256)


def column_order():
    order = np.zeros((256, 256), np.float32)
    for row in range(4):
        for core in range(2):
            for j in range(32):
                order[row * 64 + core * 32 + j, core * 128 + row * 32 + j] = 1.0
    return order


def slot_places(swap):
    places = [(i // 16, i % 16 + SHIFT) for i in range(64)]
    left = [(r, c) for r in range(4) for c in range(2)]
    right = [(r, 18 + c) for r in range(4) for c in range(2)]
    return places + (right + left if swap else left + right)


def place_tables():
    queries, keys = slot_places(False), slot_places(True)
    offsets = np.full((80, 80), 49, np.int32)
    for k, (kr, kc) in enumerate(keys):
        for q, (qr, qc) in enumerate(queries):
            if kc // 4 == qc // 4:
                offsets[k, q] = 7 * (qr - kr + 3) + (qc % 4 - kc % 4 + 3)
    fold_keys = np.zeros((32, 160), np.float32)
    for head in range(2):
        for k, (kr, kc) in enumerate(keys):
            fold_keys[head * 16 + kr * 4 + kc % 4, head * 80 + k] = 1.0
    fold_queries = np.zeros((80, 16), np.float32)
    for q, (qr, qc) in enumerate(queries):
        fold_queries[q, qr * 4 + qc % 4] = 1.0
    return offsets, fold_keys, fold_queries


def dot(a, b, ca, cb, precision=None):
    return lax.dot_general(
        a, b, (((ca,), (cb,)), ((), ())), precision=precision, preferred_element_type=F32
    )


def kernel(
    nz,
    ny,
    hd,
    model,
    factor,
    q_in,
    k_in,
    v_in,
    og_in,
    w_hbm,
    tw_hbm,
    rel_hbm,
    t_hbm,
    sel_hbm,
    offs_hbm,
    foldk_hbm,
    foldq_hbm,
    dq_out,
    dk_out,
    dv_out,
    wg_hbm,
    tg_hbm,
    bg_hbm,
    w_in,
    tw_in,
    rel_in,
    t_in,
    sel,
    offs,
    foldk,
    foldq,
    xe,
    lrx,
    snd,
    rcv,
    snd2,
    rcv2,
    yb,
    wz,
    wf,
    ge,
    gate_ref,
    emb_mine,
    bias_ref,
    prob_ref,
    probb_ref,
    dscore_ref,
    cot_ref,
    mb,
    rc,
    mc,
    rx2,
    rd,
    dsum,
    dgot,
    mz,
    rz,
    rsum,
    ry,
    dqs,
    dks,
    dvs,
    bterm,
    pay,
    ax,
    az,
    ay,
    wg_out,
    tg_out,
    bg_out,
    load_sem,
    out_sem,
    halo_s,
    halo_r,
    agy_s,
    agy_r,
    agz_s,
    agz_r,
    agx_s,
    agx_r,
    agc_s,
    agc_r,
    agd_s,
    agd_r,
    rsc_s,
    rsc_r,
    rsx_s,
    rsx_r,
    rsd_s,
    rsd_r,
    rsz_s,
    rsz_r,
    rsy_s,
    rsy_r,
    ary_s,
    ary_r,
    arz_s,
    arz_r,
    arx_s,
    arx_r,
):
    lat = lax.axis_index("lat")
    lon = lax.axis_index("lon")
    nlat, nlon = XL * nz, XH * ny * 2
    xl, z = lat // nz, lat % nz
    xh, y, core = lon // (2 * ny), (lon // 2) % ny, lon % 2
    half, quarter = model // 2, model // 4
    slabs = hd // 128
    heads = hd // 64
    width = 3 * hd + model
    og0 = 3 * hd
    groups = ny // 4

    def at(xl_, z_, xh_, y_, core_):
        return (xl_ * nz + z_, xh_ * 2 * ny + y_ * 2 + core_)

    far_z = sorted(range(1, nz), key=lambda d: -min(d, nz - d))
    far_y = sorted(range(1, ny), key=lambda d: -min(d, ny - d))
    zs = [(d, lax.rem(z + d, nz), lax.rem(z - d + nz, nz)) for d in far_z]
    xcs = [(a, b, c) for a in range(XL) for b in range(XH) for c in range(2) if a + b + c]
    ys = [(d, lax.rem(y + d, ny), lax.rem(y - d + ny, ny)) for d in far_y]
    up, down = lax.rem(lat + nlat - 1, nlat), lax.rem(lat + 1, nlat)
    left, right = lax.rem(lon + nlon - 1, nlon), lax.rem(lon + 1, nlon)

    def remote(src, dst, send, recv, device):
        return pltpu.make_async_remote_copy(
            src_ref=src,
            dst_ref=dst,
            send_sem=send,
            recv_sem=recv,
            device_id=device,
            device_id_type=MESH,
        )

    barrier = pltpu.get_barrier_semaphore()
    sibling = at(xl, z, xh, y, 1 - core)
    peers = [at(xl, z, xh, y_, core) for _, y_, _ in ys]
    peers += [at(xl, z_, xh, y, core) for _, z_, _ in zs]
    peers += [at(xl ^ a, z, xh ^ b, y, core ^ c) for a, b, c in xcs]
    peers += [(up, lon), (down, lon)]
    peers += [(i, j) for j in (left, right) for i in (lat, up, down)]
    peers += [sibling]
    for peer in peers:
        pl.semaphore_signal(barrier, inc=1, device_id=peer, device_id_type=MESH)

    loads = [
        (w_hbm, w_in),
        (q_in.at[0], xe.at[2:18, :, 0:hd]),
        (k_in.at[0], xe.at[2:18, :, hd : 2 * hd]),
        (v_in.at[0], xe.at[2:18, :, 2 * hd : og0]),
        (og_in.at[0], xe.at[2:18, :, og0:width]),
        (sel_hbm, sel),
        (t_hbm, t_in),
        (tw_hbm, tw_in),
        (rel_hbm, rel_in),
        (offs_hbm, offs),
        (foldk_hbm, foldk),
        (foldq_hbm, foldq),
    ]
    loads = [pltpu.make_async_copy(a, b, load_sem.at[i]) for i, (a, b) in enumerate(loads)]
    for load in loads:
        load.start()

    lane = lax.broadcasted_iota(jnp.int32, (32, 128), 1)
    row = lax.broadcasted_iota(jnp.int32, (32, 128), 0)
    lane0 = lax.rem(y, 4) * 32
    spread = (lane == row + lane0).astype(F32).astype(BF)
    loads[0].wait()
    yb[y] = dot(w_in[...], spread, 1, 0).astype(BF)
    pl.semaphore_wait(barrier, len(peers))

    def agy(d, y_, slot):
        return remote(yb.at[slot], yb.at[slot], agy_s.at[d], agy_r.at[d], at(xl, z, xh, y_, core))

    agy_sent = [agy(d, y_, y) for d, y_, _ in ys]
    for copy in agy_sent:
        copy.start()

    for load in loads[1:4]:
        load.wait()
    lat_qkv = [
        remote(
            xe.at[16:18, :, 0:og0], xe.at[0:2, :, 0:og0], halo_s.at[0], halo_r.at[0], (down, lon)
        ),
        remote(
            xe.at[2:4, :, 0:og0], xe.at[18:20, :, 0:og0], halo_s.at[1], halo_r.at[1], (up, lon)
        ),
    ]
    for copy in lat_qkv:
        copy.start()

    loads[4].wait()
    loads[5].wait()
    order = sel[448:704].astype(BF)

    def reorder(blocks):
        moved = [dot(block, order, 1, 0).astype(BF) for block in blocks]
        return [m[:, 0:128] for m in moved] + [m[:, 128:256] for m in moved]

    og_blocks = [
        xe[2:18, :, og0 + 256 * i : og0 + 256 * (i + 1)].reshape(256, 256)
        for i in range(model // 256)
    ]
    for i, block in enumerate(reorder(og_blocks)):
        xe[2:18, :, og0 + 128 * i : og0 + 128 * (i + 1)] = block.reshape(16, 16, 128)

    fields = [
        xe[2:18, :, 0:hd].reshape(256, hd),
        xe[2:18, :, hd : 2 * hd].reshape(256, hd),
        xe[2:18, :, og0 : og0 + half].reshape(256, hd),
        xe[2:18, :, 2 * hd : og0].reshape(256, hd),
        xe[2:18, :, og0 + half : width].reshape(256, hd),
    ]
    sq, sk = sel[0:224].astype(BF), sel[224:448].astype(BF)
    snd[:, :, 0] = (
        (dot(sq, fields[0], 1, 0) + dot(sk, fields[1], 1, 0)).astype(BF).reshape(2, 7, 16, hd)
    )
    snd[:, :, 1] = (
        (dot(sq, fields[2], 1, 0) + dot(sk, fields[3], 1, 0)).astype(BF).reshape(2, 7, 16, hd)
    )

    def strips(src, dst, base):
        devices = [
            (0, slice(0, 5), (lat, right)),
            (1, slice(0, 5), (lat, left)),
            (0, 5, (down, right)),
            (0, 6, (up, right)),
            (1, 5, (down, left)),
            (1, 6, (up, left)),
        ]
        return [
            remote(
                src.at[way, part],
                dst.at[way, part],
                halo_s.at[base + i],
                halo_r.at[base + i],
                device,
            )
            for i, (way, part, device) in enumerate(devices)
        ]

    lon_qkv = strips(snd, rcv, 2)
    for copy in lon_qkv:
        copy.start()

    snd2[...] = dot(sq, fields[4], 1, 0).astype(BF).reshape(2, 7, 16, hd)
    late = [
        remote(
            xe.at[16:18, :, og0:width],
            xe.at[0:2, :, og0:width],
            halo_s.at[8],
            halo_r.at[8],
            (down, lon),
        ),
        remote(
            xe.at[2:4, :, og0:width],
            xe.at[18:20, :, og0:width],
            halo_s.at[9],
            halo_r.at[9],
            (up, lon),
        ),
    ]
    late += strips(snd2, rcv2, 10)
    for copy in late:
        copy.start()

    for load in loads[6:]:
        load.wait()
    tval = t_in[0, 0].astype(F32)
    half_emb = tw_in.shape[0] // 2
    decay = -math.log(10000.0)
    freq = lax.broadcasted_iota(jnp.int32, (16, half_emb), 1).astype(F32)
    angle = tval * jnp.exp(decay * freq / half_emb)
    emb = jnp.concatenate([jnp.cos(angle), jnp.sin(angle)], axis=1)
    emb_hi = emb.astype(BF).astype(F32)
    emb_mid = (emb - emb_hi).astype(BF).astype(F32)
    emb_lo = emb - emb_hi - emb_mid
    emb_row = lax.broadcasted_iota(jnp.int32, (16, 2 * half_emb), 0)
    parts = jnp.where(
        emb_row == 0,
        emb_hi,
        jnp.where(emb_row == 1, emb_mid, jnp.where(emb_row == 2, emb_lo, 0.0)),
    ).astype(BF)
    tw_blocks = [tw_in[:, 256 * i : 256 * (i + 1)] for i in range(model // 256)]
    tw = jnp.concatenate(reorder(tw_blocks), axis=1)
    gate = jnp.sum(dot(parts, tw, 1, 0), axis=0, keepdims=True)
    gate_ref[...] = jnp.broadcast_to(gate, (8, model))
    emb_rows = 2 * half_emb // nlat
    index = lat * emb_rows + lax.broadcasted_iota(jnp.int32, (emb_rows, 128), 0)
    freq = lax.rem(index, half_emb).astype(F32)
    angle = tval * jnp.exp(decay * freq / half_emb)
    emb_mine[...] = jnp.where(index < half_emb, jnp.cos(angle), jnp.sin(angle))

    def bias_rows(i, carry):
        rows = pl.ds(pl.multiple_of(i * 16, 16), 16)
        code = offs[rows, :]
        acc = [jnp.full((16, 80), NEG, F32) for _ in range(heads)]
        for o in range(49):
            hit = code == o
            acc = [jnp.where(hit, rel_in[h, o], acc[h]) for h in range(heads)]
        for h in range(heads):
            bias_ref[h, rows, :] = acc[h]
        return carry

    lax.fori_loop(0, 5, bias_rows, 0)

    for d, _, ysrc in ys:
        agy(d, ysrc, ysrc).wait_recv()
    for g in range(groups):
        pair = [yb[4 * g + i] + yb[4 * g + i + 1] for i in (0, 2)]
        wz[z, :, g * 128 : (g + 1) * 128] = pair[0] + pair[1]

    def agz(d, z_, zslot):
        return remote(
            wz.at[zslot], wz.at[zslot], agz_s.at[d], agz_r.at[d], at(xl, z_, xh, y, core)
        )

    near = [(1, 0), (1, 1)]

    def columns(core_, xh_):
        return pl.ds(pl.multiple_of(core_ * half + xh_ * quarter, 128), quarter)

    def piece(xl_, xh_, core_):
        return wf.at[pl.ds(xl_ * nz, nz), :, columns(core_, xh_)]

    def neighbour(b):
        return at(1 - xl, z, xh ^ b, y, core)

    def agx(b, slot_xl, slot_xh):
        return remote(
            wz, piece(slot_xl, slot_xh, core), agx_s.at[b], agx_r.at[b], neighbour(b)
        )

    agx_sent = [agx(b, xl, xh) for _, b in near]

    far = at(xl, z, 1 - xh, y, core)

    def agf(xh_):
        block = wf.at[xl * nz + z, :, columns(core, xh_)]
        return remote(wz.at[z], block, agx_s.at[2], agx_r.at[2], far)

    def agd(d, z_, zslot):
        block = wf.at[xl * nz + zslot, :, columns(core, 1 - xh)]
        return remote(block, block, agd_s.at[d], agd_r.at[d], at(xl, z_, xh, y, core))

    agf_sent = agf(xh)
    agf_sent.start()
    agz_sent = [agz(d, z_, z) for d, z_, _ in zs]
    for copy in agz_sent:
        copy.start()

    def agc(i, xl_, xh_, core_):
        block = piece(xl_, xh_, core_)
        return remote(block, block, agc_s.at[i], agc_r.at[i], sibling)

    agc_sent = [agc(0, xl, xh, core)]

    def spread_x():
        for d, _, zsrc in zs:
            agz(d, zsrc, zsrc).wait_recv()
        for copy in agx_sent:
            copy.start()
        wf[pl.ds(xl * nz, nz), :, columns(core, xh)] = wz[...]
        agc_sent[0].start()


    edge = (y == 0) | (y == ny - 1)

    @pl.when(edge)
    def _():
        spread_x()

    for copy in lat_qkv + lon_qkv:
        copy.wait_recv()
    top = (lax.broadcasted_iota(jnp.int32, (16, hd), 0) < 8).astype(F32).astype(BF)
    bot = (lax.broadcasted_iota(jnp.int32, (16, hd), 0) >= 8).astype(F32).astype(BF)
    for wi in range(5):
        got = []
        for m in range(2):
            pair = [rcv[0, wi, m], rcv[1, wi, m]]
            if wi == 0:
                pair = [pair[0] + rcv[0, 5, m], pair[1] + rcv[1, 5, m]]
            if wi == 4:
                pair = [pair[0] + rcv[0, 6, m], pair[1] + rcv[1, 6, m]]
            got.append(pair)
        lrx[wi, :, 0:hd] = got[0][0] * top + got[0][1] * bot
        lrx[wi, :, hd : 2 * hd] = got[0][1] * top + got[0][0] * bot
        lrx[wi, :, 2 * hd : og0] = got[1][1] * top + got[1][0] * bot
        lrx[wi, :, og0 : og0 + half] = got[1][0] * top + got[1][1] * bot

    lanes = lax.broadcasted_iota(jnp.int32, (80, 128), 1)
    mask0 = (lanes < 64).astype(F32).astype(BF)
    mask1 = (lanes >= 64).astype(F32).astype(BF)
    low_lanes = lax.broadcasted_iota(jnp.int32, (64, 128), 1) < 64

    def slot_row(shape, dim):
        i = lax.broadcasted_iota(jnp.int32, shape, dim)
        return jnp.where(i < 64, i // 16, lax.rem(i, 8) // 2)

    key_row = slot_row((80, 80), 0)
    query_row = slot_row((1, 80), 1)
    query_lane = lax.broadcasted_iota(jnp.int32, (1, 80), 1)
    scale = 64 ** (-0.5)

    def group(wi, base, s):
        cols = pl.ds(pl.multiple_of(base + s * 128, 128), 128)
        own = xe[4 * wi : 4 * wi + 4, :, cols].reshape(64, 128)
        return jnp.concatenate([own, lrx[wi, :, cols]], axis=0)

    def both(x):
        return jnp.concatenate([x * mask0, x * mask1], axis=0)

    def global_row(wi, r):
        return lat * 16 - SHIFT + 4 * wi + r

    def forward(s, carry):
        attn = []
        bias = bias_ref[pl.ds(2 * s, 2)]
        for wi in range(5):
            q = group(wi, 0, s)
            kk = both(group(wi, hd, s))
            vv = both(group(wi, 2 * hd, s))
            score = (dot(kk, q, 1, 1) * scale).reshape(2, 80, 80) + bias
            if wi in (0, 4):
                rows = global_row(wi, key_row)
                score = jnp.where((rows >= 0) & (rows < nlat * 16), score, NEG)
            peak = jnp.max(score, axis=1, keepdims=True)
            expo = jnp.exp(score - peak)
            inverse = 1.0 / jnp.sum(expo, axis=1, keepdims=True)
            if wi in (0, 4):
                rows = global_row(wi, query_row)
                keep = ((rows >= 0) & (rows < nlat * 16)).astype(F32)
                inverse = inverse * keep.reshape(1, 1, 80)
            prob = (expo * inverse).reshape(160, 80)
            prob_ref[s, wi] = prob
            prob_b = prob.astype(BF)
            probb_ref[s, wi] = prob_b
            attn.append(dot(prob_b, vv, 0, 0)[0:64].astype(BF))
        attn = jnp.concatenate(attn, axis=0)[32:288]
        og = xe[2:18, :, og0:width].reshape(256, model)
        term = dot(attn, og, 0, 0).astype(BF).reshape(4, 32, model)
        mb[pl.ds(4 * s, 4)] = term
        rsc(s).start()
        return carry

    def rsc(s):
        rows = pl.ds(4 * s, 4)
        cols = pl.ds(pl.multiple_of((1 - core) * half, 128), half)
        return remote(mb.at[rows, :, cols], rc.at[rows], rsc_s.at[s], rsc_r.at[s], sibling)

    ours, theirs = xl * (slabs // 2), (1 - xl) * (slabs // 2)
    forward(ours, 0)
    agf(1 - xh).wait_recv()
    agd_sent = [agd(d, z_, z) for d, z_, _ in zs]
    for copy in agd_sent:
        copy.start()
    for i in range(1, slabs // 2):
        forward(ours + i, 0)

    @pl.when(jnp.logical_not(edge))
    def _():
        spread_x()

    def core_sum(s):
        rsc(s).wait_recv()
        rows = pl.ds(4 * s, 4)
        cols = pl.ds(pl.multiple_of(core * half, 128), half)
        mc[rows] = (mb[rows, :, cols].astype(F32) + rc[rows].astype(F32)).astype(BF)

    far_cols = pl.ds(pl.multiple_of((1 - xh) * quarter, 128), quarter)

    def rsd(d, z_, zslot):
        return remote(
            mc.at[xl * nz + z_, :, far_cols],
            rd.at[zslot],
            rsd_s.at[d],
            rsd_r.at[d],
            at(xl, z_, xh, y, core),
        )

    far_sum = remote(dsum, dgot, rsx_s.at[2], rsx_r.at[2], far)

    def rsx2(b):
        return remote(
            mc.at[pl.ds((1 - xl) * nz, nz), :, pl.ds((xh ^ b) * quarter, quarter)],
            rx2.at[b],
            rsx_s.at[b],
            rsx_r.at[b],
            neighbour(b),
        )

    forward(theirs, 0)
    for i in range(slabs // 2):
        core_sum(ours + i)
    rsd_sent = [rsd(d, z_, z) for d, z_, _ in zs]
    for copy in rsd_sent:
        copy.start()
    rd[z] = mc[xl * nz + z, :, far_cols]
    for i in range(1, slabs // 2):
        forward(theirs + i, 0)

    for _, b in near:
        agx(b, 1 - xl, xh ^ b).wait_recv()
        agc_sent.append(agc(1 + b, 1 - xl, xh ^ b, core))
        agc_sent[-1].start()

    for i in range(slabs // 2):
        core_sum(theirs + i)
    rsx_sent = [rsx2(b) for _, b in near]
    for copy in rsx_sent:
        copy.start()

    for copy in late:
        copy.wait_recv()
    gate_row = gate_ref[0:1, :]
    for wi in range(5):
        pair = [rcv2[0, wi], rcv2[1, wi]]
        if wi == 0:
            pair = [pair[0] + rcv2[0, 5], pair[1] + rcv2[1, 5]]
        if wi == 4:
            pair = [pair[0] + rcv2[0, 6], pair[1] + rcv2[1, 6]]
        lrx[wi, :, og0 + half : width] = pair[0] * top + pair[1] * bot
        own = xe[4 * wi : 4 * wi + 4, :, og0:width].reshape(64, model)
        ge[wi, 0:64] = (own.astype(F32) * gate_row).astype(BF)
        ge[wi, 64:80] = (lrx[wi, :, og0:width].astype(F32) * gate_row).astype(BF)

    def cotangent(s):
        weight = wf[pl.ds(4 * s, 2 * slabs)].reshape(64 * slabs, model)
        cot = dot(ge[...].reshape(400, model), weight, 1, 1).astype(BF)
        for i in range(slabs // 2):
            cot_ref[s + i] = cot[:, 128 * i : 128 * (i + 1)]

    def backward(s, gate_terms):
        weight = wf[pl.ds(4 * s, 4)].reshape(128, model)
        bias_sum = jnp.zeros((160, 80), F32)
        for wi in range(5):
            vv = both(group(wi, 2 * hd, s))
            prob = prob_ref[s, wi].reshape(2, 80, 80)
            dprob = dot(vv, cot_ref[s, 80 * wi : 80 * wi + 80], 1, 1).reshape(2, 80, 80)
            inner = jnp.sum(prob * dprob, axis=1, keepdims=True)
            dscore = (prob * (dprob - inner)).reshape(160, 80)
            if wi in (0, 4):
                first, last = (32, 64) if wi == 0 else (0, 32)
            else:
                first, last = 0, 64
            mine = (query_lane >= first) & (query_lane < last)
            bias_sum = bias_sum + jnp.where(mine, dscore, 0.0)
            dscore_ref[s, wi] = dscore.astype(BF)
        folded = split_dot(foldk[...].astype(BF), bias_sum)
        bterm[pl.ds(pl.multiple_of(32 * s, 32), 32), :] = dot(
            folded, foldq[...], 1, 0, lax.Precision.HIGHEST
        )
        term = mb[pl.ds(4 * s, 4)].reshape(128, model)
        product = weight.astype(F32) * term.astype(F32)
        return gate_terms + jnp.sum(product.reshape(16, 8, model), axis=0)

    def split_dot(a, b):
        high = b.astype(BF)
        return dot(a, high, 1, 0) + dot(a, (b - high.astype(F32)).astype(BF), 1, 0)

    for _, b in near:
        agc(1 + b, 1 - xl, xh ^ b, 1 - core).wait_recv()
    cotangent(theirs)
    gate_terms = backward(theirs, jnp.zeros((8, model), F32))

    for d, _, zsrc in zs:
        agd(d, zsrc, zsrc).wait_recv()
    agc_sent.append(agc(3, xl, 1 - xh, core))
    agc_sent[-1].start()
    for i in range(1, slabs // 2):
        gate_terms = backward(theirs + i, gate_terms)

    for d, _, zsrc in zs:
        rsd(d, zsrc, zsrc).wait_recv()
    total = rd[0].astype(F32)
    for j in range(1, nz):
        total = total + rd[j].astype(F32)
    dsum[...] = total.astype(BF)
    far_sum.start()
    agc(0, xl, xh, 1 - core).wait_recv()
    agc(3, xl, 1 - xh, 1 - core).wait_recv()
    cotangent(ours)
    gate_terms = lax.fori_loop(ours, ours + slabs // 2, backward, gate_terms)
    gate_terms = jnp.sum(gate_terms, axis=0, keepdims=True)

    term_row = lax.broadcasted_iota(jnp.int32, (16 * heads, 128), 0)
    key_place = lax.rem(term_row, 16)
    offset = lax.broadcasted_iota(jnp.int32, (16 * heads, 128), 1)
    by_offset = jnp.zeros((16 * heads, 128), F32)
    for p in range(16):
        goal = 7 * (p // 4 - key_place // 4 + 3) + (p % 4 - lax.rem(key_place, 4) + 3)
        by_offset = by_offset + jnp.where(offset == goal, bterm[:, p : p + 1], 0.0)
    by_offset = jnp.sum(by_offset.reshape(heads, 16, 128), axis=1)
    if heads < 8:
        by_offset = jnp.concatenate([by_offset, jnp.zeros((8 - heads, 128), F32)], axis=0)
    row = lax.broadcasted_iota(jnp.int32, (8, 128), 0)
    upper = lax.broadcasted_iota(jnp.int32, (8, 128), 1) >= 64
    for c in range(2):
        for h in range(XH):
            packed = by_offset
            for i in range(quarter // 64):
                first = c * half + h * quarter + (i // 2) * 128
                lanes_i = jnp.broadcast_to(gate_terms[:, first : first + 128], (8, 128))
                if i % 2 == 0:
                    lanes_i = pltpu.roll(lanes_i, 64, 1)
                packed = jnp.where(upper & (row == i), lanes_i, packed)
            pay[c, h] = packed

    def arx(a, b, c, slot_xl, slot_xh, slot_core, xl_, xh_, core_):
        return remote(
            pay.at[core_, xh_],
            ax.at[slot_xl * XH + slot_xh, slot_core],
            arx_s.at[a, b, c],
            arx_r.at[a, b, c],
            at(xl_, z, xh_, y, core_),
        )

    arx_sent = [arx(a, b, c, xl, xh, core, xl ^ a, xh ^ b, core ^ c) for a, b, c in xcs]
    for copy in arx_sent:
        copy.start()
    ax[xl * XH + xh, core] = pay[core, xh]

    for _, b in near:
        rsx2(b).wait_recv()
    for i in range(nz):
        total = mc[xl * nz + i, :, pl.ds(pl.multiple_of(xh * quarter, 128), quarter)].astype(F32)
        mz[i] = (total + rx2[0, i].astype(F32) + rx2[1, i].astype(F32)).astype(BF)

    def rsz(d, z_, zslot):
        return remote(mz.at[z_], rz.at[zslot], rsz_s.at[d], rsz_r.at[d], at(xl, z_, xh, y, core))

    rsz_sent = [rsz(d, z_, z) for d, z_, _ in zs]
    for copy in rsz_sent:
        copy.start()
    rz[z] = mz[z]

    def gradients(s, carry):
        cols = pl.ds(pl.multiple_of(s * 128, 128), 128)
        for wi in range(5):
            q = group(wi, 0, s)
            kk = both(group(wi, hd, s))
            c = cot_ref[s, 80 * wi : 80 * wi + 80]
            ds = dscore_ref[s, wi]
            pb = probb_ref[s, wi]
            dq = dot(ds, kk, 0, 0)[0:64] * scale
            own_ds = jnp.concatenate([ds[0:64], ds[80:144]], axis=0)
            own_pb = jnp.concatenate([pb[0:64], pb[80:144]], axis=0)
            dk = dot(own_ds, q, 1, 0) * scale
            dv = dot(own_pb, c, 1, 0)
            dk = jnp.where(low_lanes, dk[0:64], dk[64:128])
            dv = jnp.where(low_lanes, dv[0:64], dv[64:128])
            rows = slice(4 * wi, 4 * wi + 4)
            dqs[rows, :, cols] = dq.astype(BF).reshape(4, 16, 128)
            dks[rows, :, cols] = dk.astype(BF).reshape(4, 16, 128)
            dvs[rows, :, cols] = dv.astype(BF).reshape(4, 16, 128)
        return carry

    lax.fori_loop(0, slabs // 2, gradients, 0)

    for a, b, c in xcs:
        arx(a, b, c, xl ^ a, xh ^ b, core ^ c, xl, xh, core).wait_recv()
    total = ax[0, 0] + ax[0, 1]
    for j in range(1, XL * XH):
        total = total + (ax[j, 0] + ax[j, 1])
    az[z] = total

    def arz(d, z_, zslot):
        return remote(
            az.at[zslot], az.at[zslot], arz_s.at[d], arz_r.at[d], at(xl, z_, xh, y, core)
        )

    arz_sent = [arz(d, z_, z) for d, z_, _ in zs]
    for copy in arz_sent:
        copy.start()

    lax.fori_loop(slabs // 2, slabs, gradients, 0)
    outs = [
        pltpu.make_async_copy(dqs.at[2:18], dq_out.at[0], out_sem.at[0]),
        pltpu.make_async_copy(dks.at[2:18], dk_out.at[0], out_sem.at[1]),
        pltpu.make_async_copy(dvs.at[2:18], dv_out.at[0], out_sem.at[2]),
    ]
    for copy in outs:
        copy.start()

    for d, z_, zsrc in zs:
        rsz(d, zsrc, zsrc).wait_recv()
    far_sum.wait_recv()
    total = dgot[...].astype(F32)
    for j in range(nz):
        total = total + rz[j].astype(F32)
    rsum[...] = total.astype(BF)

    def rsy(d, y_, slot):
        cols = pl.ds(pl.multiple_of((y_ // 4) * 128, 128), 128)
        return remote(
            rsum.at[:, cols], ry.at[slot], rsy_s.at[d], rsy_r.at[d], at(xl, z, xh, y_, core)
        )

    rsy_sent = [rsy(d, y_, y) for d, y_, _ in ys]
    for copy in rsy_sent:
        copy.start()
    ry[y] = rsum[:, pl.ds(pl.multiple_of((y // 4) * 128, 128), 128)]

    for d, _, zsrc in zs:
        arz(d, zsrc, zsrc).wait_recv()
    total = az[0]
    for j in range(1, nz):
        total = total + az[j]
    ay[y] = total

    def ary(d, y_, slot):
        return remote(ay.at[slot], ay.at[slot], ary_s.at[d], ary_r.at[d], at(xl, z, xh, y_, core))

    ary_sent = [ary(d, y_, y) for d, y_, _ in ys]
    for copy in ary_sent:
        copy.start()

    for d, _, ysrc in ys:
        rsy(d, ysrc, ysrc).wait_recv()
    total = ry[0].astype(F32)
    for j in range(1, ny):
        total = total + ry[j].astype(F32)
    back = lax.rem(128 - lane0, 128)
    first = core * half + xh * quarter + (y // 4) * 128
    gate_mine = gate_ref[0:1, pl.ds(pl.multiple_of(first, 128), 128)]
    wg_out[...] = pltpu.roll(total * gate_mine * factor, back, 1)[:, 0:32]

    for d, _, ysrc in ys:
        ary(d, ysrc, ysrc).wait_recv()
    total = ay[0]
    for j in range(1, ny):
        total = total + ay[j]
    bg_out[...] = total[0:heads, 0:49] * factor
    gate_sum = jnp.sum(jnp.where(row == y // 2, total, 0.0), axis=0, keepdims=True) * factor
    gate_sum = pltpu.roll(jnp.broadcast_to(gate_sum, (8, 128)), 64 - lax.rem(y, 2) * 32, 1)
    tg_out[...] = (emb_mine[...] * gate_sum[0:1])[:, 0:32]

    results = [(wg_out, wg_hbm), (tg_out, tg_hbm), (bg_out, bg_hbm)]
    results = [pltpu.make_async_copy(a, b, out_sem.at[3 + i]) for i, (a, b) in enumerate(results)]
    for copy in results:
        copy.start()

    sent = lat_qkv + lon_qkv + late + agy_sent + agz_sent + agx_sent + rsx_sent
    sent += rsz_sent + rsy_sent + ary_sent + arz_sent + arx_sent
    sent += agc_sent + agd_sent + rsd_sent + [agf_sent, far_sum]
    for copy in sent:
        copy.wait_send()
    lax.fori_loop(0, slabs, lambda s, c: (rsc(s).wait_send(), c)[1], 0)
    for copy in outs + results:
        copy.wait()


def body(
    query_field, key_field, value_field, out_grad, out_weight, time_weight, rel_bias, timesteps
):
    frames, tile_rows, tile_cols, hd = query_field.shape
    model = out_grad.shape[3]
    heads = rel_bias.shape[0]
    nlat, nlon = lax.axis_size("lat"), lax.axis_size("lon")
    nz, ny = nlat // XL, nlon // (2 * XH)
    factor = 1.0 / math.sqrt(frames * tile_rows * nlat * tile_cols * nlon)
    half, quarter = model // 2, model // 4
    slabs = hd // 128
    width = 3 * hd + model
    selq, selk = strip_tables()
    order = column_order()
    offs, foldk, foldq = place_tables()
    hbm = pl.BlockSpec(memory_space=pltpu.HBM)
    small_outs = [
        jax.ShapeDtypeStruct(out_weight.shape, F32),
        jax.ShapeDtypeStruct((time_weight.shape[0] // nlat, model // nlon), F32),
        jax.ShapeDtypeStruct(rel_bias.shape, F32),
    ]
    dma = pltpu.SemaphoreType.DMA
    field = jax.ShapeDtypeStruct(query_field.shape, BF)
    sems = [dma((12,)), dma((6,))]
    for shape in (
        (16,),
        (ny,),
        (nz,),
        (3,),
        (4,),
        (nz,),
        (slabs,),
        (3,),
        (nz,),
        (nz,),
        (ny,),
        (ny,),
        (nz,),
        (XL, XH, 2),
    ):
        sems += [dma(shape), dma(shape)]
    out_shape = [field, field, field] + small_outs
    results = pl.pallas_call(
        functools.partial(kernel, nz, ny, hd, model, factor),
        out_shape=out_shape,
        in_specs=[hbm] * 12,
        out_specs=[hbm] * 6,
        scratch_shapes=[
            pltpu.VMEM(out_weight.shape, BF),
            pltpu.VMEM(time_weight.shape, BF),
            pltpu.SMEM(rel_bias.shape, F32),
            pltpu.SMEM((1, 1), jnp.int32),
            pltpu.VMEM((704, 256), F32),
            pltpu.VMEM((80, 80), jnp.int32),
            pltpu.VMEM((32, 160), F32),
            pltpu.VMEM((80, 16), F32),
            pltpu.VMEM((20, 16, width), BF),
            pltpu.VMEM((5, 16, width), BF),
            pltpu.VMEM((2, 7, 2, 16, hd), BF),
            pltpu.VMEM((2, 7, 2, 16, hd), BF),
            pltpu.VMEM((2, 7, 16, hd), BF),
            pltpu.VMEM((2, 7, 16, hd), BF),
            pltpu.VMEM((ny, 32, 128), BF),
            pltpu.VMEM((nz, 32, quarter), BF),
            pltpu.VMEM((nlat, 32, model), BF),
            pltpu.VMEM((5, 80, model), BF),
            pltpu.VMEM((8, model), F32),
            pltpu.VMEM((time_weight.shape[0] // nlat, 128), F32),
            pltpu.VMEM((heads, 80, 80), F32),
            pltpu.VMEM((slabs, 5, 160, 80), F32),
            pltpu.VMEM((slabs, 5, 160, 80), BF),
            pltpu.VMEM((slabs, 5, 160, 80), BF),
            pltpu.VMEM((slabs, 400, 128), BF),
            pltpu.VMEM((nlat, 32, model), BF),
            pltpu.VMEM((nlat, 32, half), BF),
            pltpu.VMEM((nlat, 32, half), BF),
            pltpu.VMEM((2, nz, 32, quarter), BF),
            pltpu.VMEM((nz, 32, quarter), BF),
            pltpu.VMEM((32, quarter), BF),
            pltpu.VMEM((32, quarter), BF),
            pltpu.VMEM((nz, 32, quarter), BF),
            pltpu.VMEM((nz, 32, quarter), BF),
            pltpu.VMEM((32, quarter), BF),
            pltpu.VMEM((ny, 32, 128), BF),
            pltpu.VMEM((20, 16, hd), BF),
            pltpu.VMEM((20, 16, hd), BF),
            pltpu.VMEM((20, 16, hd), BF),
            pltpu.VMEM((16 * heads, 16), F32),
            pltpu.VMEM((2, XH, 8, 128), F32),
            pltpu.VMEM((XL * XH, 2, 8, 128), F32),
            pltpu.VMEM((nz, 8, 128), F32),
            pltpu.VMEM((ny, 8, 128), F32),
        ]
        + [pltpu.VMEM(o.shape, F32) for o in small_outs]
        + sems,
        compiler_params=pltpu.CompilerParams(
            collective_id=0, has_side_effects=True, vmem_limit_bytes=VMEM_LIMIT
        ),
        cost_estimate=pl.CostEstimate(
            flops=2_000_000_000, bytes_accessed=4_000_000, transcendentals=1_000_000
        ),
    )(
        query_field,
        key_field,
        value_field,
        out_grad,
        out_weight,
        time_weight,
        rel_bias,
        timesteps.reshape(1, 1),
        jnp.asarray(np.concatenate([selq, selk, order])),
        jnp.asarray(offs),
        jnp.asarray(foldk),
        jnp.asarray(foldq),
    )
    return pl.pallas_call(
        hand_out,
        out_shape=out_shape,
        in_specs=[hbm] * 6,
        out_specs=[hbm] * 6,
        scratch_shapes=[pltpu.VMEM(o.shape, o.dtype) for o in out_shape] + [dma((2, 6))],
        compiler_params=pltpu.CompilerParams(vmem_limit_bytes=VMEM_LIMIT),
    )(*results)


def hand_out(*refs):
    sem = refs[18]
    loads = [pltpu.make_async_copy(refs[i], refs[12 + i], sem.at[0, i]) for i in range(6)]
    stores = [pltpu.make_async_copy(refs[12 + i], refs[6 + i], sem.at[1, i]) for i in range(6)]
    for load in loads:
        load.start()
    for load, store in zip(loads, stores):
        load.wait()
        store.start()
    for store in stores:
        store.wait()


def solution(mesh):
    tile = P(None, "lat", "lon", None)
    return jax.shard_map(
        body,
        mesh=mesh,
        in_specs=(tile, tile, tile, tile, P("lat", "lon"), P(), P(), P()),
        out_specs=(tile, tile, tile, P("lat", "lon"), P("lat", "lon"), P()),
        check_vma=False,
    )
```

```python
import functools
import math

import jax
import jax.numpy as jnp
import numpy as np
from jax import lax
from jax.experimental import pallas as pl
from jax.experimental.pallas import tpu as pltpu
from jax.sharding import PartitionSpec as P

SHIFT = 2
XL = 2
XH = 2
NEG = -1e9
VMEM_LIMIT = 60 * 1024 * 1024
MESH = pl.DeviceIdType.MESH
BF = jnp.bfloat16
F32 = jnp.float32


def strip_tables():
    first = np.zeros((2, 7, 16, 256), np.float32)
    second = np.zeros((2, 7, 16, 256), np.float32)
    for way, col0 in ((0, 14), (1, 0)):
        for block in range(7):
            for r in range(4):
                if block < 5:
                    row = 4 * block + r - SHIFT
                elif block == 5:
                    row = 14 + r if r < 2 else -1
                else:
                    row = r - 2 if r >= 2 else -1
                if not 0 <= row < 16:
                    continue
                for c in range(2):
                    token = row * 16 + col0 + c
                    low = r * 2 + c
                    first[way, block, low if way == 0 else low + 8, token] = 1.0
                    second[way, block, low + 8 if way == 0 else low, token] = 1.0
    return first.reshape(224, 256), second.reshape(224, 256)


def column_order():
    order = np.zeros((256, 256), np.float32)
    for row in range(4):
        for core in range(2):
            for j in range(32):
                order[row * 64 + core * 32 + j, core * 128 + row * 32 + j] = 1.0
    return order


def slot_places(swap):
    places = [(i // 16, i % 16 + SHIFT) for i in range(64)]
    left = [(r, c) for r in range(4) for c in range(2)]
    right = [(r, 18 + c) for r in range(4) for c in range(2)]
    return places + (right + left if swap else left + right)


def place_tables():
    queries, keys = slot_places(False), slot_places(True)
    offsets = np.full((80, 80), 49, np.int32)
    for k, (kr, kc) in enumerate(keys):
        for q, (qr, qc) in enumerate(queries):
            if kc // 4 == qc // 4:
                offsets[k, q] = 7 * (qr - kr + 3) + (qc % 4 - kc % 4 + 3)
    fold_keys = np.zeros((32, 160), np.float32)
    for head in range(2):
        for k, (kr, kc) in enumerate(keys):
            fold_keys[head * 16 + kr * 4 + kc % 4, head * 80 + k] = 1.0
    fold_queries = np.zeros((80, 16), np.float32)
    for q, (qr, qc) in enumerate(queries):
        fold_queries[q, qr * 4 + qc % 4] = 1.0
    return offsets, fold_keys, fold_queries


def dot(a, b, ca, cb, precision=None):
    return lax.dot_general(
        a, b, (((ca,), (cb,)), ((), ())), precision=precision, preferred_element_type=F32
    )


def kernel(
    nz,
    ny,
    hd,
    model,
    factor,
    q_in,
    k_in,
    v_in,
    og_in,
    w_hbm,
    tw_hbm,
    rel_hbm,
    t_hbm,
    sel_hbm,
    offs_hbm,
    foldk_hbm,
    foldq_hbm,
    dq_out,
    dk_out,
    dv_out,
    wg_hbm,
    tg_hbm,
    bg_hbm,
    w_in,
    tw_in,
    rel_in,
    t_in,
    sel,
    offs,
    foldk,
    foldq,
    xe,
    lrx,
    snd,
    rcv,
    snd2,
    rcv2,
    yb,
    wz,
    wf,
    ge,
    gate_ref,
    emb_mine,
    bias_ref,
    prob_ref,
    probb_ref,
    dscore_ref,
    cot_ref,
    mb,
    rc,
    mc,
    rx2,
    rd,
    dsum,
    dgot,
    mz,
    rz,
    rsum,
    ry,
    dqs,
    dks,
    dvs,
    bterm,
    pay,
    ax,
    az,
    ay,
    wg_out,
    tg_out,
    bg_out,
    load_sem,
    out_sem,
    halo_s,
    halo_r,
    agy_s,
    agy_r,
    agz_s,
    agz_r,
    agx_s,
    agx_r,
    agc_s,
    agc_r,
    agd_s,
    agd_r,
    rsc_s,
    rsc_r,
    rsx_s,
    rsx_r,
    rsd_s,
    rsd_r,
    rsz_s,
    rsz_r,
    rsy_s,
    rsy_r,
    ary_s,
    ary_r,
    arz_s,
    arz_r,
    arx_s,
    arx_r,
):
    lat = lax.axis_index("lat")
    lon = lax.axis_index("lon")
    nlat, nlon = XL * nz, XH * ny * 2
    xl, z = lat // nz, lat % nz
    xh, y, core = lon // (2 * ny), (lon // 2) % ny, lon % 2
    half, quarter = model // 2, model // 4
    slabs = hd // 128
    heads = hd // 64
    width = 3 * hd + model
    og0 = 3 * hd
    groups = ny // 4

    def at(xl_, z_, xh_, y_, core_):
        return (xl_ * nz + z_, xh_ * 2 * ny + y_ * 2 + core_)

    far_z = sorted(range(1, nz), key=lambda d: -min(d, nz - d))
    far_y = sorted(range(1, ny), key=lambda d: -min(d, ny - d))
    zs = [(d, lax.rem(z + d, nz), lax.rem(z - d + nz, nz)) for d in far_z]
    xcs = [(a, b, c) for a in range(XL) for b in range(XH) for c in range(2) if a + b + c]
    ys = [(d, lax.rem(y + d, ny), lax.rem(y - d + ny, ny)) for d in far_y]
    up, down = lax.rem(lat + nlat - 1, nlat), lax.rem(lat + 1, nlat)
    left, right = lax.rem(lon + nlon - 1, nlon), lax.rem(lon + 1, nlon)

    def remote(src, dst, send, recv, device):
        return pltpu.make_async_remote_copy(
            src_ref=src,
            dst_ref=dst,
            send_sem=send,
            recv_sem=recv,
            device_id=device,
            device_id_type=MESH,
        )

    barrier = pltpu.get_barrier_semaphore()
    sibling = at(xl, z, xh, y, 1 - core)
    peers = [at(xl, z, xh, y_, core) for _, y_, _ in ys]
    peers += [at(xl, z_, xh, y, core) for _, z_, _ in zs]
    peers += [at(xl ^ a, z, xh ^ b, y, core ^ c) for a, b, c in xcs]
    peers += [(up, lon), (down, lon)]
    peers += [(i, j) for j in (left, right) for i in (lat, up, down)]
    peers += [sibling]
    for peer in peers:
        pl.semaphore_signal(barrier, inc=1, device_id=peer, device_id_type=MESH)

    loads = [
        (w_hbm, w_in),
        (q_in.at[0], xe.at[2:18, :, 0:hd]),
        (k_in.at[0], xe.at[2:18, :, hd : 2 * hd]),
        (v_in.at[0], xe.at[2:18, :, 2 * hd : og0]),
        (og_in.at[0], xe.at[2:18, :, og0:width]),
        (sel_hbm, sel),
        (t_hbm, t_in),
        (tw_hbm, tw_in),
        (rel_hbm, rel_in),
        (offs_hbm, offs),
        (foldk_hbm, foldk),
        (foldq_hbm, foldq),
    ]
    loads = [pltpu.make_async_copy(a, b, load_sem.at[i]) for i, (a, b) in enumerate(loads)]
    for load in loads:
        load.start()

    lane = lax.broadcasted_iota(jnp.int32, (32, 128), 1)
    row = lax.broadcasted_iota(jnp.int32, (32, 128), 0)
    lane0 = lax.rem(y, 4) * 32
    spread = (lane == row + lane0).astype(F32).astype(BF)
    loads[0].wait()
    yb[y] = dot(w_in[...], spread, 1, 0).astype(BF)
    pl.semaphore_wait(barrier, len(peers))

    def agy(d, y_, slot):
        return remote(yb.at[slot], yb.at[slot], agy_s.at[d], agy_r.at[d], at(xl, z, xh, y_, core))

    agy_sent = [agy(d, y_, y) for d, y_, _ in ys]
    for copy in agy_sent:
        copy.start()

    for load in loads[1:4]:
        load.wait()
    lat_qkv = [
        remote(
            xe.at[16:18, :, 0:og0], xe.at[0:2, :, 0:og0], halo_s.at[0], halo_r.at[0], (down, lon)
        ),
        remote(
            xe.at[2:4, :, 0:og0], xe.at[18:20, :, 0:og0], halo_s.at[1], halo_r.at[1], (up, lon)
        ),
    ]
    for copy in lat_qkv:
        copy.start()

    loads[4].wait()
    loads[5].wait()
    order = sel[448:704].astype(BF)

    def reorder(blocks):
        moved = [dot(block, order, 1, 0).astype(BF) for block in blocks]
        return [m[:, 0:128] for m in moved] + [m[:, 128:256] for m in moved]

    og_blocks = [
        xe[2:18, :, og0 + 256 * i : og0 + 256 * (i + 1)].reshape(256, 256)
        for i in range(model // 256)
    ]
    for i, block in enumerate(reorder(og_blocks)):
        xe[2:18, :, og0 + 128 * i : og0 + 128 * (i + 1)] = block.reshape(16, 16, 128)

    fields = [
        xe[2:18, :, 0:hd].reshape(256, hd),
        xe[2:18, :, hd : 2 * hd].reshape(256, hd),
        xe[2:18, :, og0 : og0 + half].reshape(256, hd),
        xe[2:18, :, 2 * hd : og0].reshape(256, hd),
        xe[2:18, :, og0 + half : width].reshape(256, hd),
    ]
    sq, sk = sel[0:224].astype(BF), sel[224:448].astype(BF)
    snd[:, :, 0] = (
        (dot(sq, fields[0], 1, 0) + dot(sk, fields[1], 1, 0)).astype(BF).reshape(2, 7, 16, hd)
    )
    snd[:, :, 1] = (
        (dot(sq, fields[2], 1, 0) + dot(sk, fields[3], 1, 0)).astype(BF).reshape(2, 7, 16, hd)
    )

    def strips(src, dst, base):
        devices = [
            (0, slice(0, 5), (lat, right)),
            (1, slice(0, 5), (lat, left)),
            (0, 5, (down, right)),
            (0, 6, (up, right)),
            (1, 5, (down, left)),
            (1, 6, (up, left)),
        ]
        return [
            remote(
                src.at[way, part],
                dst.at[way, part],
                halo_s.at[base + i],
                halo_r.at[base + i],
                device,
            )
            for i, (way, part, device) in enumerate(devices)
        ]

    lon_qkv = strips(snd, rcv, 2)
    for copy in lon_qkv:
        copy.start()

    snd2[...] = dot(sq, fields[4], 1, 0).astype(BF).reshape(2, 7, 16, hd)
    late = [
        remote(
            xe.at[16:18, :, og0:width],
            xe.at[0:2, :, og0:width],
            halo_s.at[8],
            halo_r.at[8],
            (down, lon),
        ),
        remote(
            xe.at[2:4, :, og0:width],
            xe.at[18:20, :, og0:width],
            halo_s.at[9],
            halo_r.at[9],
            (up, lon),
        ),
    ]
    late += strips(snd2, rcv2, 10)
    for copy in late:
        copy.start()

    for load in loads[6:]:
        load.wait()
    tval = t_in[0, 0].astype(F32)
    half_emb = tw_in.shape[0] // 2
    decay = -math.log(10000.0)
    freq = lax.broadcasted_iota(jnp.int32, (16, half_emb), 1).astype(F32)
    angle = tval * jnp.exp(decay * freq / half_emb)
    emb = jnp.concatenate([jnp.cos(angle), jnp.sin(angle)], axis=1)
    emb_hi = emb.astype(BF).astype(F32)
    emb_mid = (emb - emb_hi).astype(BF).astype(F32)
    emb_lo = emb - emb_hi - emb_mid
    emb_row = lax.broadcasted_iota(jnp.int32, (16, 2 * half_emb), 0)
    parts = jnp.where(
        emb_row == 0,
        emb_hi,
        jnp.where(emb_row == 1, emb_mid, jnp.where(emb_row == 2, emb_lo, 0.0)),
    ).astype(BF)
    tw_blocks = [tw_in[:, 256 * i : 256 * (i + 1)] for i in range(model // 256)]
    tw = jnp.concatenate(reorder(tw_blocks), axis=1)
    gate = jnp.sum(dot(parts, tw, 1, 0), axis=0, keepdims=True)
    gate_ref[...] = jnp.broadcast_to(gate, (8, model))
    emb_rows = 2 * half_emb // nlat
    index = lat * emb_rows + lax.broadcasted_iota(jnp.int32, (emb_rows, 128), 0)
    freq = lax.rem(index, half_emb).astype(F32)
    angle = tval * jnp.exp(decay * freq / half_emb)
    emb_mine[...] = jnp.where(index < half_emb, jnp.cos(angle), jnp.sin(angle))

    def bias_rows(i, carry):
        rows = pl.ds(pl.multiple_of(i * 16, 16), 16)
        code = offs[rows, :]
        acc = [jnp.full((16, 80), NEG, F32) for _ in range(heads)]
        for o in range(49):
            hit = code == o
            acc = [jnp.where(hit, rel_in[h, o], acc[h]) for h in range(heads)]
        for h in range(heads):
            bias_ref[h, rows, :] = acc[h]
        return carry

    lax.fori_loop(0, 5, bias_rows, 0)

    for d, _, ysrc in ys:
        agy(d, ysrc, ysrc).wait_recv()
    for g in range(groups):
        pair = [yb[4 * g + i] + yb[4 * g + i + 1] for i in (0, 2)]
        wz[z, :, g * 128 : (g + 1) * 128] = pair[0] + pair[1]

    def agz(d, z_, zslot):
        return remote(
            wz.at[zslot], wz.at[zslot], agz_s.at[d], agz_r.at[d], at(xl, z_, xh, y, core)
        )

    near = [(1, 0), (1, 1)]

    def columns(core_, xh_):
        return pl.ds(pl.multiple_of(core_ * half + xh_ * quarter, 128), quarter)

    def piece(xl_, xh_, core_):
        return wf.at[pl.ds(xl_ * nz, nz), :, columns(core_, xh_)]

    def neighbour(b):
        return at(1 - xl, z, xh ^ b, y, core)

    def agx(b, slot_xl, slot_xh):
        return remote(
            wz, piece(slot_xl, slot_xh, core), agx_s.at[b], agx_r.at[b], neighbour(b)
        )

    agx_sent = [agx(b, xl, xh) for _, b in near]

    far = at(xl, z, 1 - xh, y, core)

    def agf(xh_):
        block = wf.at[xl * nz + z, :, columns(core, xh_)]
        return remote(wz.at[z], block, agx_s.at[2], agx_r.at[2], far)

    def agd(d, z_, zslot):
        block = wf.at[xl * nz + zslot, :, columns(core, 1 - xh)]
        return remote(block, block, agd_s.at[d], agd_r.at[d], at(xl, z_, xh, y, core))

    agf_sent = agf(xh)
    agf_sent.start()
    agz_sent = [agz(d, z_, z) for d, z_, _ in zs]
    for copy in agz_sent:
        copy.start()

    def agc(i, xl_, xh_, core_):
        block = piece(xl_, xh_, core_)
        return remote(block, block, agc_s.at[i], agc_r.at[i], sibling)

    agc_sent = [agc(0, xl, xh, core)]

    def spread_x():
        for d, _, zsrc in zs:
            agz(d, zsrc, zsrc).wait_recv()
        for copy in agx_sent:
            copy.start()
        wf[pl.ds(xl * nz, nz), :, columns(core, xh)] = wz[...]
        agc_sent[0].start()


    edge = (y == 0) | (y == ny - 1)

    @pl.when(edge)
    def _():
        spread_x()

    for copy in lat_qkv + lon_qkv:
        copy.wait_recv()
    top = (lax.broadcasted_iota(jnp.int32, (16, hd), 0) < 8).astype(F32).astype(BF)
    bot = (lax.broadcasted_iota(jnp.int32, (16, hd), 0) >= 8).astype(F32).astype(BF)
    for wi in range(5):
        got = []
        for m in range(2):
            pair = [rcv[0, wi, m], rcv[1, wi, m]]
            if wi == 0:
                pair = [pair[0] + rcv[0, 5, m], pair[1] + rcv[1, 5, m]]
            if wi == 4:
                pair = [pair[0] + rcv[0, 6, m], pair[1] + rcv[1, 6, m]]
            got.append(pair)
        lrx[wi, :, 0:hd] = got[0][0] * top + got[0][1] * bot
        lrx[wi, :, hd : 2 * hd] = got[0][1] * top + got[0][0] * bot
        lrx[wi, :, 2 * hd : og0] = got[1][1] * top + got[1][0] * bot
        lrx[wi, :, og0 : og0 + half] = got[1][0] * top + got[1][1] * bot

    lanes = lax.broadcasted_iota(jnp.int32, (80, 128), 1)
    mask0 = (lanes < 64).astype(F32).astype(BF)
    mask1 = (lanes >= 64).astype(F32).astype(BF)
    low_lanes = lax.broadcasted_iota(jnp.int32, (64, 128), 1) < 64

    def slot_row(shape, dim):
        i = lax.broadcasted_iota(jnp.int32, shape, dim)
        return jnp.where(i < 64, i // 16, lax.rem(i, 8) // 2)

    key_row = slot_row((80, 80), 0)
    query_row = slot_row((1, 80), 1)
    query_lane = lax.broadcasted_iota(jnp.int32, (1, 80), 1)
    scale = 64 ** (-0.5)

    def group(wi, base, s):
        cols = pl.ds(pl.multiple_of(base + s * 128, 128), 128)
        own = xe[4 * wi : 4 * wi + 4, :, cols].reshape(64, 128)
        return jnp.concatenate([own, lrx[wi, :, cols]], axis=0)

    def both(x):
        return jnp.concatenate([x * mask0, x * mask1], axis=0)

    def global_row(wi, r):
        return lat * 16 - SHIFT + 4 * wi + r

    def forward(s, carry):
        attn = []
        bias = bias_ref[pl.ds(2 * s, 2)]
        for wi in range(5):
            q = group(wi, 0, s)
            kk = both(group(wi, hd, s))
            vv = both(group(wi, 2 * hd, s))
            score = (dot(kk, q, 1, 1) * scale).reshape(2, 80, 80) + bias
            if wi in (0, 4):
                rows = global_row(wi, key_row)
                score = jnp.where((rows >= 0) & (rows < nlat * 16), score, NEG)
            peak = jnp.max(score, axis=1, keepdims=True)
            expo = jnp.exp(score - peak)
            inverse = 1.0 / jnp.sum(expo, axis=1, keepdims=True)
            if wi in (0, 4):
                rows = global_row(wi, query_row)
                keep = ((rows >= 0) & (rows < nlat * 16)).astype(F32)
                inverse = inverse * keep.reshape(1, 1, 80)
            prob = (expo * inverse).reshape(160, 80)
            prob_ref[s, wi] = prob
            prob_b = prob.astype(BF)
            probb_ref[s, wi] = prob_b
            attn.append(dot(prob_b, vv, 0, 0)[0:64].astype(BF))
        attn = jnp.concatenate(attn, axis=0)[32:288]
        og = xe[2:18, :, og0:width].reshape(256, model)
        term = dot(attn, og, 0, 0).astype(BF).reshape(4, 32, model)
        mb[pl.ds(4 * s, 4)] = term
        rsc(s).start()
        return carry

    def rsc(s):
        rows = pl.ds(4 * s, 4)
        cols = pl.ds(pl.multiple_of((1 - core) * half, 128), half)
        return remote(mb.at[rows, :, cols], rc.at[rows], rsc_s.at[s], rsc_r.at[s], sibling)

    ours, theirs = xl * (slabs // 2), (1 - xl) * (slabs // 2)
    forward(ours, 0)
    for i in range(1, slabs // 2):
        forward(ours + i, 0)

    @pl.when(jnp.logical_not(edge))
    def _():
        spread_x()

    agf(1 - xh).wait_recv()
    agd_sent = [agd(d, z_, z) for d, z_, _ in zs]
    for copy in agd_sent:
        copy.start()

    def core_sum(s):
        rsc(s).wait_recv()
        rows = pl.ds(4 * s, 4)
        cols = pl.ds(pl.multiple_of(core * half, 128), half)
        mc[rows] = (mb[rows, :, cols].astype(F32) + rc[rows].astype(F32)).astype(BF)

    far_cols = pl.ds(pl.multiple_of((1 - xh) * quarter, 128), quarter)

    def rsd(d, z_, zslot):
        return remote(
            mc.at[xl * nz + z_, :, far_cols],
            rd.at[zslot],
            rsd_s.at[d],
            rsd_r.at[d],
            at(xl, z_, xh, y, core),
        )

    far_sum = remote(dsum, dgot, rsx_s.at[2], rsx_r.at[2], far)

    def rsx2(b):
        return remote(
            mc.at[pl.ds((1 - xl) * nz, nz), :, pl.ds((xh ^ b) * quarter, quarter)],
            rx2.at[b],
            rsx_s.at[b],
            rsx_r.at[b],
            neighbour(b),
        )

    forward(theirs, 0)
    for i in range(slabs // 2):
        core_sum(ours + i)
    rsd_sent = [rsd(d, z_, z) for d, z_, _ in zs]
    for copy in rsd_sent:
        copy.start()
    rd[z] = mc[xl * nz + z, :, far_cols]
    for i in range(1, slabs // 2):
        forward(theirs + i, 0)

    for _, b in near:
        agx(b, 1 - xl, xh ^ b).wait_recv()
        agc_sent.append(agc(1 + b, 1 - xl, xh ^ b, core))
        agc_sent[-1].start()

    for i in range(slabs // 2):
        core_sum(theirs + i)
    rsx_sent = [rsx2(b) for _, b in near]
    for copy in rsx_sent:
        copy.start()

    for copy in late:
        copy.wait_recv()
    gate_row = gate_ref[0:1, :]
    for wi in range(5):
        pair = [rcv2[0, wi], rcv2[1, wi]]
        if wi == 0:
            pair = [pair[0] + rcv2[0, 5], pair[1] + rcv2[1, 5]]
        if wi == 4:
            pair = [pair[0] + rcv2[0, 6], pair[1] + rcv2[1, 6]]
        lrx[wi, :, og0 + half : width] = pair[0] * top + pair[1] * bot
        own = xe[4 * wi : 4 * wi + 4, :, og0:width].reshape(64, model)
        ge[wi, 0:64] = (own.astype(F32) * gate_row).astype(BF)
        ge[wi, 64:80] = (lrx[wi, :, og0:width].astype(F32) * gate_row).astype(BF)

    def cotangent(s):
        weight = wf[pl.ds(4 * s, 2 * slabs)].reshape(64 * slabs, model)
        cot = dot(ge[...].reshape(400, model), weight, 1, 1).astype(BF)
        for i in range(slabs // 2):
            cot_ref[s + i] = cot[:, 128 * i : 128 * (i + 1)]

    def backward(s, gate_terms):
        weight = wf[pl.ds(4 * s, 4)].reshape(128, model)
        bias_sum = jnp.zeros((160, 80), F32)
        for wi in range(5):
            vv = both(group(wi, 2 * hd, s))
            prob = prob_ref[s, wi].reshape(2, 80, 80)
            dprob = dot(vv, cot_ref[s, 80 * wi : 80 * wi + 80], 1, 1).reshape(2, 80, 80)
            inner = jnp.sum(prob * dprob, axis=1, keepdims=True)
            dscore = (prob * (dprob - inner)).reshape(160, 80)
            if wi in (0, 4):
                first, last = (32, 64) if wi == 0 else (0, 32)
            else:
                first, last = 0, 64
            mine = (query_lane >= first) & (query_lane < last)
            bias_sum = bias_sum + jnp.where(mine, dscore, 0.0)
            dscore_ref[s, wi] = dscore.astype(BF)
        folded = split_dot(foldk[...].astype(BF), bias_sum)
        bterm[pl.ds(pl.multiple_of(32 * s, 32), 32), :] = dot(
            folded, foldq[...], 1, 0, lax.Precision.HIGHEST
        )
        term = mb[pl.ds(4 * s, 4)].reshape(128, model)
        product = weight.astype(F32) * term.astype(F32)
        return gate_terms + jnp.sum(product.reshape(16, 8, model), axis=0)

    def split_dot(a, b):
        high = b.astype(BF)
        return dot(a, high, 1, 0) + dot(a, (b - high.astype(F32)).astype(BF), 1, 0)

    for _, b in near:
        agc(1 + b, 1 - xl, xh ^ b, 1 - core).wait_recv()
    cotangent(theirs)
    gate_terms = backward(theirs, jnp.zeros((8, model), F32))

    for d, _, zsrc in zs:
        agd(d, zsrc, zsrc).wait_recv()
    agc_sent.append(agc(3, xl, 1 - xh, core))
    agc_sent[-1].start()
    for i in range(1, slabs // 2):
        gate_terms = backward(theirs + i, gate_terms)

    agc(0, xl, xh, 1 - core).wait_recv()
    agc(3, xl, 1 - xh, 1 - core).wait_recv()
    cotangent(ours)
    gate_terms = lax.fori_loop(ours, ours + slabs // 2, backward, gate_terms)
    gate_terms = jnp.sum(gate_terms, axis=0, keepdims=True)

    term_row = lax.broadcasted_iota(jnp.int32, (16 * heads, 128), 0)
    key_place = lax.rem(term_row, 16)
    offset = lax.broadcasted_iota(jnp.int32, (16 * heads, 128), 1)
    by_offset = jnp.zeros((16 * heads, 128), F32)
    for p in range(16):
        goal = 7 * (p // 4 - key_place // 4 + 3) + (p % 4 - lax.rem(key_place, 4) + 3)
        by_offset = by_offset + jnp.where(offset == goal, bterm[:, p : p + 1], 0.0)
    by_offset = jnp.sum(by_offset.reshape(heads, 16, 128), axis=1)
    if heads < 8:
        by_offset = jnp.concatenate([by_offset, jnp.zeros((8 - heads, 128), F32)], axis=0)
    row = lax.broadcasted_iota(jnp.int32, (8, 128), 0)
    upper = lax.broadcasted_iota(jnp.int32, (8, 128), 1) >= 64
    for c in range(2):
        for h in range(XH):
            packed = by_offset
            for i in range(quarter // 64):
                first = c * half + h * quarter + (i // 2) * 128
                lanes_i = jnp.broadcast_to(gate_terms[:, first : first + 128], (8, 128))
                if i % 2 == 0:
                    lanes_i = pltpu.roll(lanes_i, 64, 1)
                packed = jnp.where(upper & (row == i), lanes_i, packed)
            pay[c, h] = packed

    def arx(a, b, c, slot_xl, slot_xh, slot_core, xl_, xh_, core_):
        return remote(
            pay.at[core_, xh_],
            ax.at[slot_xl * XH + slot_xh, slot_core],
            arx_s.at[a, b, c],
            arx_r.at[a, b, c],
            at(xl_, z, xh_, y, core_),
        )

    arx_sent = [arx(a, b, c, xl, xh, core, xl ^ a, xh ^ b, core ^ c) for a, b, c in xcs]
    for copy in arx_sent:
        copy.start()
    ax[xl * XH + xh, core] = pay[core, xh]

    for d, _, zsrc in zs:
        rsd(d, zsrc, zsrc).wait_recv()
    total = rd[0].astype(F32)
    for j in range(1, nz):
        total = total + rd[j].astype(F32)
    dsum[...] = total.astype(BF)
    far_sum.start()

    for _, b in near:
        rsx2(b).wait_recv()
    for i in range(nz):
        total = mc[xl * nz + i, :, pl.ds(pl.multiple_of(xh * quarter, 128), quarter)].astype(F32)
        mz[i] = (total + rx2[0, i].astype(F32) + rx2[1, i].astype(F32)).astype(BF)

    def rsz(d, z_, zslot):
        return remote(mz.at[z_], rz.at[zslot], rsz_s.at[d], rsz_r.at[d], at(xl, z_, xh, y, core))

    rsz_sent = [rsz(d, z_, z) for d, z_, _ in zs]
    for copy in rsz_sent:
        copy.start()
    rz[z] = mz[z]

    def gradients(s, carry):
        cols = pl.ds(pl.multiple_of(s * 128, 128), 128)
        for wi in range(5):
            q = group(wi, 0, s)
            kk = both(group(wi, hd, s))
            c = cot_ref[s, 80 * wi : 80 * wi + 80]
            ds = dscore_ref[s, wi]
            pb = probb_ref[s, wi]
            dq = dot(ds, kk, 0, 0)[0:64] * scale
            own_ds = jnp.concatenate([ds[0:64], ds[80:144]], axis=0)
            own_pb = jnp.concatenate([pb[0:64], pb[80:144]], axis=0)
            dk = dot(own_ds, q, 1, 0) * scale
            dv = dot(own_pb, c, 1, 0)
            dk = jnp.where(low_lanes, dk[0:64], dk[64:128])
            dv = jnp.where(low_lanes, dv[0:64], dv[64:128])
            rows = slice(4 * wi, 4 * wi + 4)
            dqs[rows, :, cols] = dq.astype(BF).reshape(4, 16, 128)
            dks[rows, :, cols] = dk.astype(BF).reshape(4, 16, 128)
            dvs[rows, :, cols] = dv.astype(BF).reshape(4, 16, 128)
        return carry

    lax.fori_loop(0, slabs // 2, gradients, 0)

    for a, b, c in xcs:
        arx(a, b, c, xl ^ a, xh ^ b, core ^ c, xl, xh, core).wait_recv()
    total = ax[0, 0] + ax[0, 1]
    for j in range(1, XL * XH):
        total = total + (ax[j, 0] + ax[j, 1])
    az[z] = total

    def arz(d, z_, zslot):
        return remote(
            az.at[zslot], az.at[zslot], arz_s.at[d], arz_r.at[d], at(xl, z_, xh, y, core)
        )

    arz_sent = [arz(d, z_, z) for d, z_, _ in zs]
    for copy in arz_sent:
        copy.start()

    lax.fori_loop(slabs // 2, slabs, gradients, 0)
    outs = [
        pltpu.make_async_copy(dqs.at[2:18], dq_out.at[0], out_sem.at[0]),
        pltpu.make_async_copy(dks.at[2:18], dk_out.at[0], out_sem.at[1]),
        pltpu.make_async_copy(dvs.at[2:18], dv_out.at[0], out_sem.at[2]),
    ]
    for copy in outs:
        copy.start()

    for d, z_, zsrc in zs:
        rsz(d, zsrc, zsrc).wait_recv()
    far_sum.wait_recv()
    total = dgot[...].astype(F32)
    for j in range(nz):
        total = total + rz[j].astype(F32)
    rsum[...] = total.astype(BF)

    def rsy(d, y_, slot):
        cols = pl.ds(pl.multiple_of((y_ // 4) * 128, 128), 128)
        return remote(
            rsum.at[:, cols], ry.at[slot], rsy_s.at[d], rsy_r.at[d], at(xl, z, xh, y_, core)
        )

    rsy_sent = [rsy(d, y_, y) for d, y_, _ in ys]
    for copy in rsy_sent:
        copy.start()
    ry[y] = rsum[:, pl.ds(pl.multiple_of((y // 4) * 128, 128), 128)]

    for d, _, zsrc in zs:
        arz(d, zsrc, zsrc).wait_recv()
    total = az[0]
    for j in range(1, nz):
        total = total + az[j]
    ay[y] = total

    def ary(d, y_, slot):
        return remote(ay.at[slot], ay.at[slot], ary_s.at[d], ary_r.at[d], at(xl, z, xh, y_, core))

    ary_sent = [ary(d, y_, y) for d, y_, _ in ys]
    for copy in ary_sent:
        copy.start()

    for d, _, ysrc in ys:
        rsy(d, ysrc, ysrc).wait_recv()
    total = ry[0].astype(F32)
    for j in range(1, ny):
        total = total + ry[j].astype(F32)
    back = lax.rem(128 - lane0, 128)
    first = core * half + xh * quarter + (y // 4) * 128
    gate_mine = gate_ref[0:1, pl.ds(pl.multiple_of(first, 128), 128)]
    wg_out[...] = pltpu.roll(total * gate_mine * factor, back, 1)[:, 0:32]

    for d, _, ysrc in ys:
        ary(d, ysrc, ysrc).wait_recv()
    total = ay[0]
    for j in range(1, ny):
        total = total + ay[j]
    bg_out[...] = total[0:heads, 0:49] * factor
    gate_sum = jnp.sum(jnp.where(row == y // 2, total, 0.0), axis=0, keepdims=True) * factor
    gate_sum = pltpu.roll(jnp.broadcast_to(gate_sum, (8, 128)), 64 - lax.rem(y, 2) * 32, 1)
    tg_out[...] = (emb_mine[...] * gate_sum[0:1])[:, 0:32]

    results = [(wg_out, wg_hbm), (tg_out, tg_hbm), (bg_out, bg_hbm)]
    results = [pltpu.make_async_copy(a, b, out_sem.at[3 + i]) for i, (a, b) in enumerate(results)]
    for copy in results:
        copy.start()

    sent = lat_qkv + lon_qkv + late + agy_sent + agz_sent + agx_sent + rsx_sent
    sent += rsz_sent + rsy_sent + ary_sent + arz_sent + arx_sent
    sent += agc_sent + agd_sent + rsd_sent + [agf_sent, far_sum]
    for copy in sent:
        copy.wait_send()
    lax.fori_loop(0, slabs, lambda s, c: (rsc(s).wait_send(), c)[1], 0)
    for copy in outs + results:
        copy.wait()


def body(
    query_field, key_field, value_field, out_grad, out_weight, time_weight, rel_bias, timesteps
):
    frames, tile_rows, tile_cols, hd = query_field.shape
    model = out_grad.shape[3]
    heads = rel_bias.shape[0]
    nlat, nlon = lax.axis_size("lat"), lax.axis_size("lon")
    nz, ny = nlat // XL, nlon // (2 * XH)
    factor = 1.0 / math.sqrt(frames * tile_rows * nlat * tile_cols * nlon)
    half, quarter = model // 2, model // 4
    slabs = hd // 128
    width = 3 * hd + model
    selq, selk = strip_tables()
    order = column_order()
    offs, foldk, foldq = place_tables()
    hbm = pl.BlockSpec(memory_space=pltpu.HBM)
    small_outs = [
        jax.ShapeDtypeStruct(out_weight.shape, F32),
        jax.ShapeDtypeStruct((time_weight.shape[0] // nlat, model // nlon), F32),
        jax.ShapeDtypeStruct(rel_bias.shape, F32),
    ]
    dma = pltpu.SemaphoreType.DMA
    field = jax.ShapeDtypeStruct(query_field.shape, BF)
    sems = [dma((12,)), dma((6,))]
    for shape in (
        (16,),
        (ny,),
        (nz,),
        (3,),
        (4,),
        (nz,),
        (slabs,),
        (3,),
        (nz,),
        (nz,),
        (ny,),
        (ny,),
        (nz,),
        (XL, XH, 2),
    ):
        sems += [dma(shape), dma(shape)]
    out_shape = [field, field, field] + small_outs
    results = pl.pallas_call(
        functools.partial(kernel, nz, ny, hd, model, factor),
        out_shape=out_shape,
        in_specs=[hbm] * 12,
        out_specs=[hbm] * 6,
        scratch_shapes=[
            pltpu.VMEM(out_weight.shape, BF),
            pltpu.VMEM(time_weight.shape, BF),
            pltpu.SMEM(rel_bias.shape, F32),
            pltpu.SMEM((1, 1), jnp.int32),
            pltpu.VMEM((704, 256), F32),
            pltpu.VMEM((80, 80), jnp.int32),
            pltpu.VMEM((32, 160), F32),
            pltpu.VMEM((80, 16), F32),
            pltpu.VMEM((20, 16, width), BF),
            pltpu.VMEM((5, 16, width), BF),
            pltpu.VMEM((2, 7, 2, 16, hd), BF),
            pltpu.VMEM((2, 7, 2, 16, hd), BF),
            pltpu.VMEM((2, 7, 16, hd), BF),
            pltpu.VMEM((2, 7, 16, hd), BF),
            pltpu.VMEM((ny, 32, 128), BF),
            pltpu.VMEM((nz, 32, quarter), BF),
            pltpu.VMEM((nlat, 32, model), BF),
            pltpu.VMEM((5, 80, model), BF),
            pltpu.VMEM((8, model), F32),
            pltpu.VMEM((time_weight.shape[0] // nlat, 128), F32),
            pltpu.VMEM((heads, 80, 80), F32),
            pltpu.VMEM((slabs, 5, 160, 80), F32),
            pltpu.VMEM((slabs, 5, 160, 80), BF),
            pltpu.VMEM((slabs, 5, 160, 80), BF),
            pltpu.VMEM((slabs, 400, 128), BF),
            pltpu.VMEM((nlat, 32, model), BF),
            pltpu.VMEM((nlat, 32, half), BF),
            pltpu.VMEM((nlat, 32, half), BF),
            pltpu.VMEM((2, nz, 32, quarter), BF),
            pltpu.VMEM((nz, 32, quarter), BF),
            pltpu.VMEM((32, quarter), BF),
            pltpu.VMEM((32, quarter), BF),
            pltpu.VMEM((nz, 32, quarter), BF),
            pltpu.VMEM((nz, 32, quarter), BF),
            pltpu.VMEM((32, quarter), BF),
            pltpu.VMEM((ny, 32, 128), BF),
            pltpu.VMEM((20, 16, hd), BF),
            pltpu.VMEM((20, 16, hd), BF),
            pltpu.VMEM((20, 16, hd), BF),
            pltpu.VMEM((16 * heads, 16), F32),
            pltpu.VMEM((2, XH, 8, 128), F32),
            pltpu.VMEM((XL * XH, 2, 8, 128), F32),
            pltpu.VMEM((nz, 8, 128), F32),
            pltpu.VMEM((ny, 8, 128), F32),
        ]
        + [pltpu.VMEM(o.shape, F32) for o in small_outs]
        + sems,
        compiler_params=pltpu.CompilerParams(
            collective_id=0, has_side_effects=True, vmem_limit_bytes=VMEM_LIMIT
        ),
        cost_estimate=pl.CostEstimate(
            flops=2_000_000_000, bytes_accessed=4_000_000, transcendentals=1_000_000
        ),
    )(
        query_field,
        key_field,
        value_field,
        out_grad,
        out_weight,
        time_weight,
        rel_bias,
        timesteps.reshape(1, 1),
        jnp.asarray(np.concatenate([selq, selk, order])),
        jnp.asarray(offs),
        jnp.asarray(foldk),
        jnp.asarray(foldq),
    )
    return pl.pallas_call(
        hand_out,
        out_shape=out_shape,
        in_specs=[hbm] * 6,
        out_specs=[hbm] * 6,
        scratch_shapes=[pltpu.VMEM(o.shape, o.dtype) for o in out_shape] + [dma((2, 6))],
        compiler_params=pltpu.CompilerParams(vmem_limit_bytes=VMEM_LIMIT),
    )(*results)


def hand_out(*refs):
    sem = refs[18]
    loads = [pltpu.make_async_copy(refs[i], refs[12 + i], sem.at[0, i]) for i in range(6)]
    stores = [pltpu.make_async_copy(refs[12 + i], refs[6 + i], sem.at[1, i]) for i in range(6)]
    for load in loads:
        load.start()
    for load, store in zip(loads, stores):
        load.wait()
        store.start()
    for store in stores:
        store.wait()


def solution(mesh):
    tile = P(None, "lat", "lon", None)
    return jax.shard_map(
        body,
        mesh=mesh,
        in_specs=(tile, tile, tile, tile, P("lat", "lon"), P(), P(), P()),
        out_specs=(tile, tile, tile, P("lat", "lon"), P("lat", "lon"), P()),
        check_vma=False,
    )
```
